32 devices in a mesh: dp: 2 (over core), expert: 16 (over z, y, x).
Axes of the slice: x: 2, y: 2, z: 4, core: 2. Of those that a mesh axis runs over, the one named last changes fastest.
Arguments:
- tokens: bfloat16 [32, 1024, 768], P(('dp', 'expert')), may hold values from -6 to 6
- lengths: int32 [32], P(('dp', 'expert')), may hold values from 1 to 1024, 24576 in all
- expert_ids: int32 [32, 1024, 1], P(('dp', 'expert')), may hold values from 0 to 15; in each aligned block of 1024 rows (0 to 1023, 1024 to 2047, ..., all dimensions but the last counted through in order) at most 96 rows name the same one
- w_qkv: bfloat16 [768, 2304], replicated, may hold values from -0.21875 to 0.21875
- w_out: bfloat16 [768, 768], replicated, may hold values from -1.75 to 1.75
- norm1_gain: float32 [768], replicated, may hold values from 0.5 to 1.5
- norm2_gain: float32 [768], replicated, may hold values from 0.5 to 1.5
- w_in: bfloat16 [16, 768, 3072], P('expert'), may hold values from -0.21875 to 0.21875
- w_back: bfloat16 [16, 3072, 768], P('expert'), may hold values from -0.25 to 0.25
- cotangent: bfloat16 [32, 1024, 768], P(('dp', 'expert')), may hold values from -6 to 6
Outputs:
- output: float32 [32, 1024, 768], P(('dp', 'expert'))
- tokens_grad: float32 [32, 1024, 768], P(('dp', 'expert'))
- w_qkv_grad: float32 [768, 2304], replicated
- w_out_grad: float32 [768, 768], replicated
- norm1_gain_grad: float32 [768], replicated
- norm2_gain_grad: float32 [768], replicated
- w_in_grad: float32 [16, 768, 3072], P('expert')
- w_back_grad: float32 [16, 3072, 768], P('expert')
The draws below stay inside these ranges and needn't reach their ends.
Inputs may be any that keep to these rules, and one draw needn't show every extreme that they name: `lengths`: each sequence's live tokens are its first ones; the longest sequence fills all 1024 positions. `expert_ids`: among the 1024 positions of one sequence, padded ones included, no expert is named more than 96 times, and in some sequence one expert is named exactly 96 times.
All inputs are finite; a program needn't handle non-finite values. No bound on the sum of `lengths` on one device may be relied on, other than what follows from the above.
Results may differ from the reference program's by a relative error of at most 0.012.
Values may be sent and summed in bfloat16 or wider, within the bound.
A program may use at most 256 MiB of HBM per device.

```python
import math
import jax
import jax.numpy as jnp
import numpy as np
from jax import lax

D = 768
HEADS = 12
HEAD = 64
FF = 3072
SEQ_LEN = 1024
SEQS = 32
EXPERTS = 16
CAP = 96


def block_levels(rng, extent, shards, low, largest):
    factor_of = 1.0
    for position, shards_of in shards:
        draws = jax.random.uniform(jax.random.fold_in(jax.random.fold_in(rng, 6), position), (shards_of,), jnp.float32, low / len(shards), largest / len(shards))
        factor_of = factor_of * jnp.repeat(jnp.exp(draws), extent[position] // shards_of).reshape((-1,) + (1,) * (len(extent) - 1 - position))
    return factor_of


def profile(amount, total, bound, lean):
    loads = [(1 << 20) // math.isqrt(standing ** lean) + 1 for standing in range(2, amount + 1)]
    surplus, counts = total - bound - (amount - 1), [1] * (amount - 1)
    while surplus > 0:
        free = [i for i in range(amount - 1) if counts[i] < bound]
        mass, budget = sum([loads[i] for i in free]), surplus
        for i in free:
            extra = min(bound - counts[i], max(1, budget * loads[i] // mass), surplus)
            counts[i] = counts[i] + extra
            surplus = surplus - extra
    return np.array([bound] + counts)


def ragged_sizes(stream_key, amount, total, most, skew):
    if amount == 2:
        one = jax.random.randint(stream_key, (), max(1, total - most), min(most, total - 1) + 1)
        return jnp.stack([one, total - one])
    tallies = jnp.asarray(profile(amount, total, most, skew), jnp.int32)
    twos = (amount - 1) // 2
    source_of, taker = tallies[1:1 + 2 * twos:2], tallies[2:2 + 2 * twos:2]
    margin = jnp.minimum(source_of - 1, most - taker)
    moved = jax.random.randint(jax.random.fold_in(stream_key, 1), (twos,), 0, 1 << 20) % (margin + 1)
    tallies = tallies.at[1:1 + 2 * twos:2].set(source_of - moved).at[2:2 + 2 * twos:2].set(taker + moved)
    return tallies[jax.random.permutation(jax.random.fold_in(stream_key, 2), amount)]


def deal_out(rng, own, number, rows, number_of, top, limit, slope):
    order = jax.random.permutation(rng, number_of)
    crowded, usual = portions_of(number_of, rows * top, limit, slope, True), portions_of(number_of, rows * top, limit, slope, False)
    places = jnp.arange(number_of)

    def named(sizes, turn):
        used = int((sizes > 0).sum())
        fixed = max(1, used // 4)
        moved = fixed + (places - fixed + turn * (used - fixed)) % max(1, number_of - fixed)
        return jnp.zeros((number_of,), jnp.int32).at[order[jnp.where(places < fixed, places, moved)]].set(jnp.asarray(sizes, jnp.int32))

    sizes = jnp.where(number % 4 == 0, named(crowded, number // 4), named(usual, number - number // 4 - 1))
    mixed = jax.random.permutation(jax.random.fold_in(own, 3), number_of)
    source_of, sink = mixed[0:number_of // 2 * 2:2], mixed[1:number_of // 2 * 2:2]
    slack = jnp.minimum(sizes[source_of] - 1, limit - sizes[sink]) // 2
    slack = jnp.where((source_of == order[0]) | (sink == order[0]) | (sizes[sink] == 0), 0, jnp.maximum(slack, 0))
    moved = jax.random.randint(jax.random.fold_in(own, 4), (number_of // 2,), 0, 1 << 20) % (slack + 1)
    sizes = sizes.at[source_of].add(-moved).at[sink].add(moved)
    items = jnp.searchsorted(jnp.cumsum(sizes), jnp.arange(rows * top), side="right").astype(jnp.int32)
    grid = items.reshape(top, rows).T
    grid = grid[jax.random.permutation(jax.random.fold_in(own, 1), rows)]
    turn = jax.random.randint(jax.random.fold_in(own, 2), (rows, 1), 0, top)
    return jnp.take_along_axis(grid, (jnp.arange(top)[None, :] + turn) % top, axis=1)


def portions_of(count, total, bound, lean, full):
    weights = [(1 << 20) // math.isqrt(grade ** lean) + 1 for grade in range(1, count + 1)]
    largest = bound if full else min(bound, max(-(-total // count), total * weights[0] // sum(weights)))
    least = 1 if total - largest >= count - 1 else 0
    holding, spare = [largest] + [least] * (count - 1), total - largest - least * (count - 1)
    while spare > 0:
        candidates = [i for i in range(1, count) if holding[i] < largest] or [i for i in range(1, count) if holding[i] < bound]
        pool, budget = sum([weights[i] for i in candidates]), spare
        for i in candidates:
            addition = min(bound - holding[i], max(1, budget * weights[i] // pool), spare)
            holding[i] = holding[i] + addition
            spare = spare - addition
    return np.array(holding)


def normal_values(key, extent, deviation, most, split=(), kind=jnp.bfloat16):
    result = deviation * jax.random.normal(key, extent, jnp.float32)
    if split:
        result = result * block_levels(key, extent, split, -0.22, 0.18)
    return jnp.clip(result, -most, most).astype(kind)


def setup_inputs(seed: int = 0) -> dict:
    splits = jax.random.split(jax.random.key(seed), 11)
    tokens = normal_values(splits[0], (SEQS, SEQ_LEN, D), 1.0, 6.0, ((0, 32),))
    lengths = ragged_sizes(splits[1], SEQS, SEQS * SEQ_LEN * 3 // 4, SEQ_LEN, 0).astype(jnp.int32)
    expert_ids_keys = jax.random.split(jax.random.fold_in(splits[2], 1), SEQS * SEQ_LEN // SEQ_LEN)
    expert_ids_turns = jax.random.permutation(jax.random.fold_in(splits[2], 3), SEQS * SEQ_LEN // SEQ_LEN)
    expert_ids = jax.vmap(lambda own, number: deal_out(jax.random.fold_in(splits[2], 2), own, number, SEQ_LEN, EXPERTS, 1, CAP, 0))(expert_ids_keys, expert_ids_turns).reshape((SEQS, SEQ_LEN, 1))
    w_qkv = normal_values(splits[3], (D, 3 * D), D ** -0.5, 0.21875)
    w_out = normal_values(splits[4], (D, D), (max(D // 64, 12)) ** -0.5, 1.75)
    norm1_gain = jnp.clip(1.0 + 0.1 * jax.random.normal(splits[5], (D,), jnp.float32), 0.5, 1.5)
    norm2_gain = jnp.clip(1.0 + 0.1 * jax.random.normal(splits[6], (D,), jnp.float32), 0.5, 1.5)
    w_in = normal_values(splits[7], (EXPERTS, D, FF), D ** -0.5, 0.21875, ((0, 16),))
    w_back = normal_values(splits[8], (EXPERTS, FF, D), (FF // 6) ** -0.5, 0.25, ((0, 16),))
    cotangent = normal_values(splits[9], (SEQS, SEQ_LEN, D), 1.0, 6.0, ((0, 32),))
    return dict(tokens=tokens, lengths=lengths, expert_ids=expert_ids, w_qkv=w_qkv, w_out=w_out, norm1_gain=norm1_gain, norm2_gain=norm2_gain, w_in=w_in, w_back=w_back, cotangent=cotangent)


epsilon = 1e-05
top_precision_level = lax.Precision.HIGHEST

@jax.custom_vjp
def low(v):
    return lax.optimization_barrier(v.astype(jnp.bfloat16)).astype(jnp.float32)

@jax.custom_vjp
def low_back(v):
    return v

def low_keep(v):
    return (low(v), None)

def low_pass(kept, grad):
    return (grad,)

def back_keep(v):
    return (v, None)

def back_low(kept, grad):
    return (low(grad),)
low.defvjp(low_keep, low_pass)
low_back.defvjp(back_keep, back_low)

def layer_norm(values, gain):
    center = values - lax.optimization_barrier(jnp.mean(values, axis=-1, keepdims=True))
    variance = lax.optimization_barrier(jnp.mean(center * center, axis=-1, keepdims=True))
    return center * lax.rsqrt(variance + epsilon) * gain

def attend(packed):
    projected_output, seq_length = packed
    positions = projected_output.shape[0]
    queries = projected_output[:, :D].reshape(positions, HEADS, HEAD)
    key_heads = projected_output[:, D:2 * D].reshape(positions, HEADS, HEAD)
    value_heads = projected_output[:, 2 * D:].reshape(positions, HEADS, HEAD)
    scores = low_back(jnp.einsum('qhd,khd->hqk', queries, key_heads, precision=top_precision_level) * HEAD ** (-0.5))
    row_index = lax.broadcasted_iota(jnp.int32, scores.shape, 1)
    col_index = lax.broadcasted_iota(jnp.int32, scores.shape, 2)
    allowed = (col_index <= row_index) & (col_index < seq_length.astype(jnp.int32))
    scores = jnp.where(allowed, scores, -1e+30)
    attention_weights = low(jax.nn.softmax(scores, axis=-1))
    mixed_heads = jnp.einsum('hqk,khd->qhd', attention_weights, value_heads, precision=top_precision_level)
    return mixed_heads.reshape(positions, D)

def expert_apply(packed):
    arriving, first_weight, second_weight = packed
    pre_act = low_back(jnp.dot(arriving, first_weight, precision=top_precision_level))
    hidden = low(jax.nn.silu(pre_act))
    return low(jnp.dot(hidden, second_weight, precision=top_precision_level))

def reference(tokens, lengths, expert_ids, w_qkv, w_out, norm1_gain, norm2_gain, w_in, w_back, cotangent):
    positions = jnp.arange(SEQ_LEN, dtype=jnp.int32)
    is_live = positions[None, :] < lengths.astype(jnp.int32)[:, None]
    owner_ids = expert_ids[:, :, 0].astype(jnp.int32)
    choose = ((owner_ids[:, :, None] == jnp.arange(EXPERTS, dtype=jnp.int32)[None, None, :]) & is_live[:, :, None]).astype(jnp.int32)
    running = jnp.cumsum(choose, axis=1, dtype=jnp.int32)
    ranking = lax.optimization_barrier(jnp.sum(running * choose, axis=2, dtype=jnp.int32)) - 1
    seq_base = jnp.arange(SEQS, dtype=jnp.int32)[:, None] * CAP
    slot_index = jnp.where(is_live, owner_ids * (SEQS * CAP) + seq_base + ranking, EXPERTS * SEQS * CAP).reshape(-1).astype(jnp.int32)

    def forward(input_tokens, query_key_value_weight, output_weight, gain_one, gain_two, first_weights, second_weights):
        normalized_rows = low(layer_norm(input_tokens, gain_one))
        projected_output = low(low_back(jnp.einsum('oyp,pv->oyv', normalized_rows, query_key_value_weight, precision=top_precision_level)))
        mixed_output = low(low_back(lax.map(jax.checkpoint(attend), (projected_output, lengths.astype(jnp.int32)))))
        residual_stream = input_tokens + low_back(jnp.einsum('oyp,pv->oyv', mixed_output, output_weight, precision=top_precision_level))
        expert_in = low(low_back(layer_norm(residual_stream, gain_two))).reshape(-1, D)
        buffer = jnp.zeros((EXPERTS * SEQS * CAP + 1, D), jnp.float32).at[slot_index].add(expert_in)
        buffer = buffer[:-1].reshape(EXPERTS, SEQS * CAP, D)
        produced = lax.map(jax.checkpoint(expert_apply), (buffer, first_weights, second_weights))
        produced = jnp.concatenate([produced.reshape(-1, D), jnp.zeros((1, D), jnp.float32)], axis=0)
        return residual_stream + produced[slot_index].reshape(SEQS, SEQ_LEN, D)
    output, pullback = jax.vjp(forward, tokens.astype(jnp.float32), w_qkv.astype(jnp.float32), w_out.astype(jnp.float32), norm1_gain.astype(jnp.float32), norm2_gain.astype(jnp.float32), w_in.astype(jnp.float32), w_back.astype(jnp.float32))
    grads = pullback(cotangent.astype(jnp.float32))
    return (output, grads[0], grads[1], grads[2], grads[3], grads[4], grads[5], grads[6])
```

```python
import functools

import jax
import jax.numpy as jnp
from jax import lax
from jax.experimental import pallas as pl
from jax.experimental.pallas import tpu as pltpu
from jax.sharding import PartitionSpec as P

BF, F32, I32 = jnp.bfloat16, jnp.float32, jnp.int32
HEAD = 64
LANES = 128
ROWS = 256
EPS = 1e-5
NEG = -1e30
VMEM = pl.BlockSpec(memory_space=pltpu.VMEM)
SMEM = pl.BlockSpec(memory_space=pltpu.SMEM)
MIB = 2**20


def dot(a, b):
    return lax.dot_general(a, b, (((1,), (0,)), ((), ())), preferred_element_type=F32)


def dot_t(a, b):
    return lax.dot_general(a, b, (((1,), (1,)), ((), ())), preferred_element_type=F32)


def tdot(a, b):
    return lax.dot_general(a, b, (((0,), (0,)), ((), ())), preferred_element_type=F32)


def rows_of(i, n=ROWS):
    return pl.ds(pl.multiple_of(i * n, n), n)


def normalize(x):
    center = x - jnp.mean(x, axis=-1, keepdims=True)
    inverse = lax.rsqrt(jnp.mean(center * center, axis=-1, keepdims=True) + EPS)
    return center * inverse, inverse


def norm_back(u, hat, inverse):
    return inverse * (
        u - jnp.mean(u, axis=-1, keepdims=True) - hat * jnp.mean(u * hat, axis=-1, keepdims=True)
    )


def lane_iota(shape):
    return lax.broadcasted_iota(I32, shape, len(shape) - 1)


def split_parts(x):
    high = x.astype(BF)
    rest = x - high.astype(F32)
    middle = rest.astype(BF)
    low = (rest - middle.astype(F32)).astype(BF)
    return high, middle, low


def aug_of(x, one):
    high, middle, low = split_parts(x)
    lane = lane_iota(x.shape) % HEAD
    parts = jnp.where(
        lane == 0,
        -high.astype(F32),
        jnp.where(
            lane == 1,
            -middle.astype(F32),
            jnp.where(lane == 2, -low.astype(F32), jnp.where(lane == 3, one, 0.0)),
        ),
    )
    return parts.astype(BF)


def key_aug(seq, length):
    lane = lane_iota((seq, LANES)) % HEAD
    row = lax.broadcasted_iota(I32, (seq, LANES), 0)
    dead = jnp.where(row < length, 0.0, NEG)
    return jnp.where(lane < 3, 1.0, jnp.where(lane == 3, dead, 0.0)).astype(BF)


def forward_kernel(
    experts, capacity,
    len_ref, tok_ref, eid_row_ref, eid_col_ref, wqkv_ref, wout_ref, g1_ref, g2_ref,
    normed_ref, qkv_ref, mixed_ref, laug_ref, h_ref, slots_ref, slot_col_ref,
    kaug_ref, xin_ref, slot_row_ref,
):
    seq, width = tok_ref.shape
    blocks, pairs = seq // ROWS, width // LANES
    length = len_ref[0]

    @pl.loop(0, blocks)
    def _(i):
        hat, _ = normalize(tok_ref[rows_of(i), :].astype(F32))
        normed_ref[rows_of(i), :] = (hat * g1_ref[...]).astype(BF)

    @pl.loop(0, 3 * pairs // 2)
    def _(j):
        w = wqkv_ref[:, rows_of(j, 2 * LANES)]
        for i in range(blocks):
            r = slice(i * ROWS, (i + 1) * ROWS)
            out = dot(normed_ref[r, :], w).astype(BF)
            qkv_ref[2 * j, r, :] = out[:, :LANES]
            qkv_ref[2 * j + 1, r, :] = out[:, LANES:]

    kaug_ref[...] = key_aug(seq, length)
    first = lane_iota((1, LANES)) < HEAD
    scale = jnp.asarray(HEAD**-0.5, BF)

    @pl.loop(0, pairs)
    def _(p):
        qaug = jnp.where(lane_iota((ROWS, LANES)) % HEAD == 3, 1.0, 0.0).astype(BF)
        causal = lane_iota((ROWS, ROWS)) <= lax.broadcasted_iota(I32, (ROWS, ROWS), 0)
        one = jnp.ones((1, LANES), BF)
        for i in range(blocks):
            r = slice(i * ROWS, (i + 1) * ROWS)
            n = (i + 1) * ROWS
            q = qkv_ref[p, r, :] * scale
            k = qkv_ref[pairs + p, :n, :]
            v = qkv_ref[2 * pairs + p, :n, :]
            aug = kaug_ref[:n, :]
            outs, tops = [], []
            for head in range(2):
                mine = first if head == 0 else ~first
                s = dot_t(jnp.where(mine, q, qaug), jnp.where(mine, k, aug))
                last = jnp.where(causal, s[:, n - ROWS :], NEG)
                s = jnp.concatenate([s[:, : n - ROWS], last], axis=1) if i else last
                top = jnp.max(s, axis=1, keepdims=True)
                e = jnp.exp(s - top).astype(BF)
                outs.append(dot(e, jnp.where(mine, v, one)))
                tops.append(top)
            above = jnp.where(first, outs[0], outs[1])
            below = jnp.where(first, outs[1], outs[0])
            mixed_ref[r, rows_of(p, LANES)] = (above / pltpu.roll(below, HEAD, 1)).astype(BF)
            lse = jnp.where(first, tops[1], tops[0]) + jnp.log(below)
            laug_ref[p, r, :] = aug_of(lse, 1.0)

    @pl.loop(0, blocks)
    def _(i):
        r = rows_of(i)
        h = tok_ref[r, :].astype(F32) + dot(mixed_ref[r, :], wout_ref[...])
        h_ref[r, :] = h
        hat, _ = normalize(h)
        xin_ref[r, :] = (hat * g2_ref[...]).astype(BF)

    tri = jnp.where(
        lax.broadcasted_iota(I32, (seq, seq), 0) <= lane_iota((seq, seq)), 1.0, 0.0
    ).astype(BF)
    eid = eid_row_ref[...]
    live = lane_iota((1, seq)) < length
    pick = (lax.broadcasted_iota(I32, (experts, seq), 0) == eid) & live
    pick = jnp.where(pick, 1.0, 0.0)
    rank = jnp.sum(dot(pick.astype(BF), tri) * pick, axis=0, keepdims=True).astype(I32) - 1
    slot_row_ref[...] = jnp.where(live, eid * capacity + rank, experts * capacity)

    eid = eid_col_ref[...]
    live = lax.broadcasted_iota(I32, (seq, 1), 0) < length
    pick = (lane_iota((seq, LANES)) == eid) & live
    pick = jnp.where(pick, 1.0, 0.0)
    rank = jnp.sum(tdot(tri, pick.astype(BF)) * pick, axis=1, keepdims=True).astype(I32) - 1
    slot_col_ref[...] = jnp.where(live, eid * capacity + rank, experts * capacity)

    total = experts * capacity
    step = 4 * capacity

    @pl.loop(0, total // step)
    def _(c):
        place(slot_row_ref, xin_ref, slots_ref, c, step)


def place(slot_row_ref, src_ref, slots_ref, c, step):
    seq = src_ref.shape[0]
    index = lax.broadcasted_iota(I32, (step, seq), 0) + c * step
    onehot = jnp.where(index == slot_row_ref[...], 1.0, 0.0).astype(BF)
    slots_ref[rows_of(c, step), :] = dot(onehot, src_ref[...]).astype(BF)


def collect(slot_col_ref, ret_ref, r):
    total = ret_ref.shape[0]
    onehot = jnp.where(slot_col_ref[r, :] == lane_iota((ROWS, total)), 1.0, 0.0).astype(BF)
    return dot(onehot, ret_ref[...])


def place_kernel(experts, capacity, len_ref, eid_row_ref, cot_ref, slots_ref, slot_row_ref):
    seq, _ = cot_ref.shape
    length = len_ref[0]
    tri = jnp.where(
        lax.broadcasted_iota(I32, (seq, seq), 0) <= lane_iota((seq, seq)), 1.0, 0.0
    ).astype(BF)
    eid = eid_row_ref[...]
    live = lane_iota((1, seq)) < length
    pick = (lax.broadcasted_iota(I32, (experts, seq), 0) == eid) & live
    pick = jnp.where(pick, 1.0, 0.0)
    rank = jnp.sum(dot(pick.astype(BF), tri) * pick, axis=0, keepdims=True).astype(I32) - 1
    slot_row_ref[...] = jnp.where(live, eid * capacity + rank, experts * capacity)
    total = experts * capacity
    step = 4 * capacity

    @pl.loop(0, total // step)
    def _(c):
        place(slot_row_ref, cot_ref, slots_ref, c, step)


def collect_kernel(h_ref, slot_col_ref, ret_ref, out_ref):
    @pl.loop(0, h_ref.shape[0] // ROWS)
    def _(i):
        r = rows_of(i)
        out_ref[r, :] = h_ref[r, :] + collect(slot_col_ref, ret_ref, r)


def expert_kernel(x_ref, g_ref, win_ref, wback_ref, ffn_ref, ing_ref, wing_ref, wbg_ref, ffn_acc, ing_acc):
    t = pl.program_id(0)
    total = x_ref.shape[0]
    tile = win_ref.shape[1]
    blocks = 4
    size = total // blocks

    @pl.when(t == 0)
    def _():
        ffn_acc[...] = jnp.zeros_like(ffn_acc)
        ing_acc[...] = jnp.zeros_like(ing_acc)

    hidden_parts, act_parts = [], []
    for i in range(blocks):
        r = slice(i * size, (i + 1) * size)
        a = dot(x_ref[r, :], win_ref[...])
        gate = jax.nn.sigmoid(a)
        hidden = (a * gate).astype(BF)
        back = dot_t(g_ref[r, :], wback_ref[...])
        act = (back * gate * (1.0 + a * (1.0 - gate))).astype(BF)
        ffn_acc[r, :] += dot(hidden, wback_ref[...])
        ing_acc[r, :] += dot_t(act, win_ref[...])
        hidden_parts.append(hidden)
        act_parts.append(act)
    wing_ref[...] = tdot(x_ref[...], jnp.concatenate(act_parts, axis=0)).astype(BF)
    wbg_ref[...] = tdot(jnp.concatenate(hidden_parts, axis=0), g_ref[...]).astype(BF)

    @pl.when(t == pl.num_programs(0) - 1)
    def _():
        ffn_ref[...] = ffn_acc[...].astype(BF)
        ing_ref[...] = ing_acc[...].astype(BF)


def backward_kernel(
    len_ref, tok_ref, cot_ref, normed_ref, qkv_ref, mixed_ref, laug_ref, h_ref, ret_ref, slot_col_ref,
    wqkv_ref, wout_ref, g1_ref, g2_ref,
    tokg_ref, wqkvg_ref, woutg_ref, g1g_ref, g2g_ref,
    hgrad_ref, hg_ref, mg_ref, daug_ref, kaug_ref, dq_ref, qg_ref, normt_ref,
):
    seq, width = tok_ref.shape
    blocks, pairs = seq // ROWS, width // LANES
    g1g_ref[...] = jnp.zeros_like(g1g_ref)
    g2g_ref[...] = jnp.zeros_like(g2g_ref)
    first = lane_iota((1, LANES)) < HEAD

    @pl.loop(0, blocks)
    def _(i):
        r = rows_of(i)
        hat, inverse = normalize(h_ref[r, :])
        ing = collect(slot_col_ref, ret_ref, r)
        g2g_ref[...] += jnp.sum(ing * hat, axis=0, keepdims=True)
        grad = cot_ref[r, :].astype(F32) + norm_back(ing * g2_ref[...], hat, inverse)
        hgrad_ref[r, :] = grad
        low = grad.astype(BF)
        hg_ref[r, :] = low
        mg = dot_t(low, wout_ref[...]).astype(BF)
        for p in range(pairs):
            part = mg[:, p * LANES : (p + 1) * LANES]
            mg_ref[p, r, :] = part
            prod = part.astype(F32) * mixed_ref[r, p * LANES : (p + 1) * LANES].astype(F32)
            zero = jnp.zeros_like(prod)
            d0 = jnp.sum(jnp.where(first, prod, zero), axis=1, keepdims=True)
            d1 = jnp.sum(jnp.where(first, zero, prod), axis=1, keepdims=True)
            daug_ref[p, r, :] = aug_of(jnp.where(first, d1, d0), 0.0)
        normt_ref[:, r] = normed_ref[r, :].T

    woutg_ref[...] = tdot(mixed_ref[...], hg_ref[...]).astype(BF)
    kaug_ref[...] = key_aug(seq, len_ref[0])
    scale = jnp.asarray(HEAD**-0.5, BF)

    @pl.loop(0, pairs)
    def _(p):
        keep = lane_iota((ROWS, ROWS)) >= lax.broadcasted_iota(I32, (ROWS, ROWS), 0)
        vaug = jnp.where(lane_iota((ROWS, LANES)) % HEAD < 3, 1.0, 0.0).astype(BF)
        none = jnp.zeros((ROWS, LANES), BF)
        dq_ref[...] = jnp.zeros_like(dq_ref)
        for j in range(blocks):
            kr = slice(j * ROWS, (j + 1) * ROWS)
            qr = slice(j * ROWS, seq)
            q = qkv_ref[p, qr, :] * scale
            k = qkv_ref[pairs + p, kr, :]
            v = qkv_ref[2 * pairs + p, kr, :]
            do = mg_ref[p, qr, :]
            la, da = laug_ref[p, qr, :], daug_ref[p, qr, :]
            ka = kaug_ref[kr, :]
            dvs, dks, dss, kms = [], [], [], []
            for head in range(2):
                mine = first if head == 0 else ~first
                s = dot_t(jnp.where(mine, k, ka), jnp.where(mine, q, la))
                e = jnp.exp(s)
                start = jnp.where(keep, e[:, :ROWS], 0.0)
                e = jnp.concatenate([start, e[:, ROWS:]], axis=1) if j < blocks - 1 else start
                dp = dot_t(jnp.where(mine, v, vaug), jnp.where(mine, do, da))
                ds = (e * dp).astype(BF)
                dvs.append(dot(e.astype(BF), do))
                dks.append(dot(ds, q))
                dss.append(ds)
                kms.append(jnp.where(mine, k, none))
            qg_ref[kr, rows_of(2 * pairs + p, LANES)] = jnp.where(first, dvs[0], dvs[1]).astype(BF)
            qg_ref[kr, rows_of(pairs + p, LANES)] = jnp.where(first, dks[0], dks[1]).astype(BF)
            dq_ref[qr, :] += tdot(jnp.concatenate(dss, axis=0), jnp.concatenate(kms, axis=0))
        qg_ref[:, rows_of(p, LANES)] = (dq_ref[...] * HEAD**-0.5).astype(BF)

    @pl.loop(0, 3 * pairs // 2)
    def _(j):
        c = rows_of(j, 2 * LANES)
        wqkvg_ref[:, c] = dot(normt_ref[...], qg_ref[:, c]).astype(BF)

    @pl.loop(0, blocks)
    def _(i):
        r = rows_of(i)
        n1 = dot_t(qg_ref[r, :], wqkv_ref[...])
        hat, inverse = normalize(tok_ref[r, :].astype(F32))
        g1g_ref[...] += jnp.sum(n1 * hat, axis=0, keepdims=True)
        tokg_ref[r, :] = hgrad_ref[r, :] + norm_back(n1 * g1_ref[...], hat, inverse)


def params(mib, **kw):
    return pltpu.CompilerParams(vmem_limit_bytes=mib * MIB, **kw)


def sds(shape, dtype):
    return jax.ShapeDtypeStruct(shape, dtype)


def shards(experts, tokens, lengths, expert_ids, w_qkv, w_out, norm1_gain, norm2_gain, w_in, w_back, cotangent):
    x, g = tokens[0], cotangent[0]
    seq, width = x.shape
    pairs = width // LANES
    capacity = 3 * seq // (2 * experts)
    capacity = (capacity + 15) // 16 * 16
    total = experts * capacity
    eid_row = expert_ids.reshape(1, seq)
    eid_col = expert_ids[0]
    g1, g2 = norm1_gain.reshape(1, width), norm2_gain.reshape(1, width)
    ff = w_in.shape[2]

    g_slots, _ = pl.pallas_call(
        functools.partial(place_kernel, experts, capacity),
        out_shape=(sds((total, width), BF), sds((1, seq), I32)),
        in_specs=[SMEM, VMEM, VMEM],
        out_specs=(VMEM, VMEM),
        compiler_params=params(40),
        name="place_gradient",
    )(lengths, eid_row, g)
    g_in = exchange(g_slots, experts)

    normed, qkv, mixed, laug, h, x_slots, slot_col = pl.pallas_call(
        functools.partial(forward_kernel, experts, capacity),
        out_shape=(
            sds((seq, width), BF),
            sds((3 * pairs, seq, LANES), BF),
            sds((seq, width), BF),
            sds((pairs, seq, LANES), BF),
            sds((seq, width), F32),
            sds((total, width), BF),
            sds((seq, 1), I32),
        ),
        in_specs=[SMEM] + [VMEM] * 7,
        out_specs=(VMEM,) * 7,
        scratch_shapes=[
            pltpu.VMEM((seq, LANES), BF),
            pltpu.VMEM((seq, width), BF),
            pltpu.VMEM((1, seq), I32),
        ],
        compiler_params=params(58),
        cost_estimate=pl.CostEstimate(flops=40 * 10**9, bytes_accessed=24 * 10**6, transcendentals=0),
        name="attention_forward",
    )(lengths, x, eid_row, eid_col, w_qkv, w_out, g1, g2)
    x_in = exchange(x_slots, experts)

    tile = 512
    full = pl.BlockSpec((total, width), lambda t: (0, 0))
    ffn, ing, wing, wbg = pl.pallas_call(
        expert_kernel,
        grid=(ff // tile,),
        out_shape=(
            sds((total, width), BF),
            sds((total, width), BF),
            sds((width, ff), BF),
            sds((ff, width), BF),
        ),
        in_specs=[
            full,
            full,
            pl.BlockSpec((width, tile), lambda t: (0, t)),
            pl.BlockSpec((tile, width), lambda t: (t, 0)),
        ],
        out_specs=(
            full,
            full,
            pl.BlockSpec((width, tile), lambda t: (0, t)),
            pl.BlockSpec((tile, width), lambda t: (t, 0)),
        ),
        scratch_shapes=[pltpu.VMEM((total, width), F32)] * 2,
        compiler_params=params(58),
        cost_estimate=pl.CostEstimate(flops=44 * 10**9, bytes_accessed=30 * 10**6, transcendentals=0),
        name="experts",
    )(x_in, g_in, w_in[0], w_back[0])
    ing_ret = exchange(ing, experts)
    ffn_ret = exchange(ffn, experts)

    tokg, wqkvg, woutg, g1g, g2g = pl.pallas_call(
        backward_kernel,
        out_shape=(
            sds((seq, width), F32),
            sds((width, 3 * width), BF),
            sds((width, width), BF),
            sds((1, width), F32),
            sds((1, width), F32),
        ),
        in_specs=[SMEM] + [VMEM] * 13,
        out_specs=(VMEM,) * 5,
        scratch_shapes=[
            pltpu.VMEM((seq, width), F32),
            pltpu.VMEM((seq, width), BF),
            pltpu.VMEM((pairs, seq, LANES), BF),
            pltpu.VMEM((pairs, seq, LANES), BF),
            pltpu.VMEM((seq, LANES), BF),
            pltpu.VMEM((seq, LANES), F32),
            pltpu.VMEM((seq, 3 * width), BF),
            pltpu.VMEM((width, seq), BF),
        ],
        compiler_params=params(60),
        cost_estimate=pl.CostEstimate(flops=60 * 10**9, bytes_accessed=24 * 10**6, transcendentals=0),
        name="attention_backward",
    )(lengths, x, g, normed, qkv, mixed, laug, h, ing_ret, slot_col, w_qkv, w_out, g1, g2)

    output = pl.pallas_call(
        collect_kernel,
        out_shape=sds((seq, width), F32),
        in_specs=[VMEM] * 3,
        out_specs=VMEM,
        compiler_params=params(40),
        name="collect_output",
    )(h, slot_col, ffn_ret)

    in_sum = lax.psum(wing, "dp").astype(F32)
    back_sum = lax.psum(wbg, "dp").astype(F32)
    both = ("dp", "expert")
    out_sum = lax.psum(woutg, both).astype(F32)
    qkv_sum = lax.psum(wqkvg, both).astype(F32)
    g1_sum, g2_sum = lax.psum((g1g[0], g2g[0]), both)
    return (
        output[None], tokg[None], qkv_sum, out_sum, g1_sum, g2_sum, in_sum[None], back_sum[None],
    )


def exchange(rows, experts):
    total, width = rows.shape
    rows = rows.reshape(experts, total // experts, width)
    return lax.all_to_all(rows, "expert", split_axis=0, concat_axis=0, tiled=True).reshape(total, width)


def solution(mesh):
    split = P(("dp", "expert"), None, None)
    mine = P("expert", None, None)
    return jax.shard_map(
        functools.partial(shards, mesh.shape["expert"]),
        mesh=mesh,
        in_specs=(split, P(("dp", "expert")), split, P(), P(), P(), P(), mine, mine, split),
        out_specs=(split, split, P(), P(), P(), P(), mine, mine),
        check_vma=False,
    )
```

```python
import functools

import jax
import jax.numpy as jnp
from jax import lax
from jax.experimental import pallas as pl
from jax.experimental.pallas import tpu as pltpu
from jax.sharding import PartitionSpec as P

BF, F32, I32 = jnp.bfloat16, jnp.float32, jnp.int32
HEAD = 64
LANES = 128
ROWS = 256
EPS = 1e-5
NEG = -1e30
VMEM = pl.BlockSpec(memory_space=pltpu.VMEM)
ANY = pl.BlockSpec(memory_space=pl.ANY)
MESH = pl.DeviceIdType.MESH
SMEM = pl.BlockSpec(memory_space=pltpu.SMEM)
MIB = 2**20


def dot(a, b):
    return lax.dot_general(a, b, (((1,), (0,)), ((), ())), preferred_element_type=F32)


def dot_t(a, b):
    return lax.dot_general(a, b, (((1,), (1,)), ((), ())), preferred_element_type=F32)


def tdot(a, b):
    return lax.dot_general(a, b, (((0,), (0,)), ((), ())), preferred_element_type=F32)


def rows_of(i, n=ROWS):
    return pl.ds(pl.multiple_of(i * n, n), n)


def normalize(x):
    center = x - jnp.mean(x, axis=-1, keepdims=True)
    inverse = lax.rsqrt(jnp.mean(center * center, axis=-1, keepdims=True) + EPS)
    return center * inverse, inverse


def norm_back(u, hat, inverse):
    return inverse * (
        u - jnp.mean(u, axis=-1, keepdims=True) - hat * jnp.mean(u * hat, axis=-1, keepdims=True)
    )


def lane_iota(shape):
    return lax.broadcasted_iota(I32, shape, len(shape) - 1)


def split_parts(x):
    high = x.astype(BF)
    rest = x - high.astype(F32)
    middle = rest.astype(BF)
    low = (rest - middle.astype(F32)).astype(BF)
    return high, middle, low


def aug_of(x, one):
    high, middle, low = split_parts(x)
    lane = lane_iota(x.shape) % HEAD
    parts = jnp.where(
        lane == 0,
        -high.astype(F32),
        jnp.where(
            lane == 1,
            -middle.astype(F32),
            jnp.where(lane == 2, -low.astype(F32), jnp.where(lane == 3, one, 0.0)),
        ),
    )
    return parts.astype(BF)


def key_aug(seq, length):
    lane = lane_iota((seq, LANES)) % HEAD
    row = lax.broadcasted_iota(I32, (seq, LANES), 0)
    dead = jnp.where(row < length, 0.0, NEG)
    return jnp.where(lane < 3, 1.0, jnp.where(lane == 3, dead, 0.0)).astype(BF)


def forward_kernel(
    experts, capacity,
    len_ref, tok_ref, eid_row_ref, eid_col_ref, wqkv_ref, wout_ref, g1_ref, g2_ref,
    normed_ref, qkv_ref, mixed_ref, laug_ref, h_ref, slots_ref, slot_col_ref,
    kaug_ref, xin_ref, slot_row_ref,
):
    seq, width = tok_ref.shape
    blocks, pairs = seq // ROWS, width // LANES
    length = len_ref[0]

    @pl.loop(0, blocks)
    def _(i):
        hat, _ = normalize(tok_ref[rows_of(i), :].astype(F32))
        normed_ref[rows_of(i), :] = (hat * g1_ref[...]).astype(BF)

    @pl.loop(0, 3 * pairs // 2)
    def _(j):
        w = wqkv_ref[:, rows_of(j, 2 * LANES)]
        for i in range(blocks):
            r = slice(i * ROWS, (i + 1) * ROWS)
            out = dot(normed_ref[r, :], w).astype(BF)
            qkv_ref[2 * j, r, :] = out[:, :LANES]
            qkv_ref[2 * j + 1, r, :] = out[:, LANES:]

    kaug_ref[...] = key_aug(seq, length)
    first = lane_iota((1, LANES)) < HEAD
    scale = jnp.asarray(HEAD**-0.5, BF)

    @pl.loop(0, pairs)
    def _(p):
        qaug = jnp.where(lane_iota((ROWS, LANES)) % HEAD == 3, 1.0, 0.0).astype(BF)
        causal = lane_iota((ROWS, ROWS)) <= lax.broadcasted_iota(I32, (ROWS, ROWS), 0)
        one = jnp.ones((1, LANES), BF)
        for i in range(blocks):
            r = slice(i * ROWS, (i + 1) * ROWS)
            n = (i + 1) * ROWS
            q = qkv_ref[p, r, :] * scale
            k = qkv_ref[pairs + p, :n, :]
            v = qkv_ref[2 * pairs + p, :n, :]
            aug = kaug_ref[:n, :]
            outs, tops = [], []
            for head in range(2):
                mine = first if head == 0 else ~first
                s = dot_t(jnp.where(mine, q, qaug), jnp.where(mine, k, aug))
                last = jnp.where(causal, s[:, n - ROWS :], NEG)
                s = jnp.concatenate([s[:, : n - ROWS], last], axis=1) if i else last
                top = jnp.max(s, axis=1, keepdims=True)
                e = jnp.exp(s - top).astype(BF)
                outs.append(dot(e, jnp.where(mine, v, one)))
                tops.append(top)
            above = jnp.where(first, outs[0], outs[1])
            below = jnp.where(first, outs[1], outs[0])
            mixed_ref[r, rows_of(p, LANES)] = (above / pltpu.roll(below, HEAD, 1)).astype(BF)
            lse = jnp.where(first, tops[1], tops[0]) + jnp.log(below)
            laug_ref[p, r, :] = aug_of(lse, 1.0)

    @pl.loop(0, blocks)
    def _(i):
        r = rows_of(i)
        h = tok_ref[r, :].astype(F32) + dot(mixed_ref[r, :], wout_ref[...])
        h_ref[r, :] = h
        hat, _ = normalize(h)
        xin_ref[r, :] = (hat * g2_ref[...]).astype(BF)

    tri = jnp.where(
        lax.broadcasted_iota(I32, (seq, seq), 0) <= lane_iota((seq, seq)), 1.0, 0.0
    ).astype(BF)
    eid = eid_row_ref[...]
    live = lane_iota((1, seq)) < length
    pick = (lax.broadcasted_iota(I32, (experts, seq), 0) == eid) & live
    pick = jnp.where(pick, 1.0, 0.0)
    rank = jnp.sum(dot(pick.astype(BF), tri) * pick, axis=0, keepdims=True).astype(I32) - 1
    slot_row_ref[...] = jnp.where(live, eid * capacity + rank, experts * capacity)

    eid = eid_col_ref[...]
    live = lax.broadcasted_iota(I32, (seq, 1), 0) < length
    pick = (lane_iota((seq, LANES)) == eid) & live
    pick = jnp.where(pick, 1.0, 0.0)
    rank = jnp.sum(tdot(tri, pick.astype(BF)) * pick, axis=1, keepdims=True).astype(I32) - 1
    slot_col_ref[...] = jnp.where(live, eid * capacity + rank, experts * capacity)

    total = experts * capacity
    step = 4 * capacity

    @pl.loop(0, total // step)
    def _(c):
        place(slot_row_ref, xin_ref, slots_ref, c, step)


def place(slot_row_ref, src_ref, slots_ref, c, step):
    seq = src_ref.shape[0]
    index = lax.broadcasted_iota(I32, (step, seq), 0) + c * step
    onehot = jnp.where(index == slot_row_ref[...], 1.0, 0.0).astype(BF)
    slots_ref[rows_of(c, step), :] = dot(onehot, src_ref[...]).astype(BF)


def collect(slot_col_ref, ret_ref, r):
    total = ret_ref.shape[0]
    onehot = jnp.where(slot_col_ref[r, :] == lane_iota((ROWS, total)), 1.0, 0.0).astype(BF)
    return dot(onehot, ret_ref[...])


def place_kernel(experts, capacity, len_ref, eid_row_ref, cot_ref, slots_ref, slot_row_ref):
    seq, _ = cot_ref.shape
    length = len_ref[0]
    tri = jnp.where(
        lax.broadcasted_iota(I32, (seq, seq), 0) <= lane_iota((seq, seq)), 1.0, 0.0
    ).astype(BF)
    eid = eid_row_ref[...]
    live = lane_iota((1, seq)) < length
    pick = (lax.broadcasted_iota(I32, (experts, seq), 0) == eid) & live
    pick = jnp.where(pick, 1.0, 0.0)
    rank = jnp.sum(dot(pick.astype(BF), tri) * pick, axis=0, keepdims=True).astype(I32) - 1
    slot_row_ref[...] = jnp.where(live, eid * capacity + rank, experts * capacity)
    total = experts * capacity
    step = 4 * capacity

    @pl.loop(0, total // step)
    def _(c):
        place(slot_row_ref, cot_ref, slots_ref, c, step)


def collect_kernel(h_ref, slot_col_ref, ret_ref, out_ref):
    @pl.loop(0, h_ref.shape[0] // ROWS)
    def _(i):
        r = rows_of(i)
        out_ref[r, :] = h_ref[r, :] + collect(slot_col_ref, ret_ref, r)


def flip(v, j, size):
    out, bit = 0, 1
    while bit < size:
        out = out + bit * ((v // bit + j // bit) % 2)
        bit *= 2
    return out


def greet(experts, with_partner):
    me = lax.axis_index("expert")
    barrier = pltpu.get_barrier_semaphore()

    @pl.loop(1, experts)
    def _(j):
        pl.semaphore_signal(
            barrier, inc=1, device_id={"expert": flip(me, j, experts)}, device_id_type=MESH
        )

    if with_partner:
        pl.semaphore_signal(
            barrier, inc=1, device_id={"dp": 1 - lax.axis_index("dp")}, device_id_type=MESH
        )
    pl.semaphore_wait(barrier, experts - 1 + int(with_partner))


def expert_kernel(
    experts, capacity,
    x_ref, g_ref, win_hbm, wback_hbm,
    ing_ref, ffn_ref, wing_ref, wbg_ref,
    xin, gin, win, wback, hidden, act, ing_out, xt, own_in, own_back, got_in, got_back,
    x_send, x_recv, r_send, r_recv, g_sem, w_sem, own_sem, ffn_sem, t_send, t_recv, o_sem,
):
    me = lax.axis_index("expert")
    other = 1 - lax.axis_index("dp")
    width, ff = win.shape
    groups, chunk = experts // 4, 4 * capacity

    def block(j):
        return pl.ds(pl.multiple_of(j * capacity, 16), capacity)

    def x_copy(j):
        peer = flip(me, j, experts)
        return pltpu.make_async_remote_copy(
            src_ref=x_ref.at[block(peer)], dst_ref=xin.at[block(j)],
            send_sem=x_send.at[j], recv_sem=x_recv.at[j],
            device_id={"expert": peer}, device_id_type=MESH,
        )

    def r_copy(j):
        return pltpu.make_async_remote_copy(
            src_ref=ing_out.at[block(j)], dst_ref=ing_ref.at[block(me)],
            send_sem=r_send.at[j], recv_sem=r_recv.at[j],
            device_id={"expert": flip(me, j, experts)}, device_id_type=MESH,
        )

    def g_copy(j):
        return pltpu.make_async_copy(g_ref.at[block(flip(me, j, experts))], gin.at[block(j)], g_sem.at[j])

    own_x = pltpu.make_async_copy(x_ref.at[block(me)], xin.at[block(0)], own_sem.at[0])
    own_ing = pltpu.make_async_copy(ing_out.at[block(0)], ing_ref.at[block(me)], own_sem.at[1])
    load_in = pltpu.make_async_copy(win_hbm, win, w_sem.at[0])
    load_back = pltpu.make_async_copy(wback_hbm, wback, w_sem.at[1])
    own_x.start()
    load_in.start()
    load_back.start()

    @pl.loop(0, experts)
    def _(j):
        g_copy(j).start()

    greet(experts, True)
    for low, high in ((2, 3), (0, 2), (3, 4)):

        @pl.loop(max(1, experts * low // 4), experts * high // 4)
        def _(j):
            x_copy(j).start()

    own_x.wait()
    load_in.wait()
    load_back.wait()

    @pl.loop(0, experts)
    def _(j):
        g_copy(j).wait()

    def ffn_copy(j):
        peer = flip(me, j, experts)
        return pltpu.make_async_copy(xin.at[block(j)], ffn_ref.at[block(peer)], ffn_sem.at[j])

    @pl.loop(0, groups)
    def _(i):
        r = rows_of(i, chunk)
        for c in range(4):
            j = 4 * i + c

            @pl.when(j > 0)
            def _():
                x_copy(j).wait_recv()

        @pl.loop(0, ff // 512)
        def _(t):
            c = rows_of(t, 512)
            a = dot(xin[r, :], win[:, c])
            gate = jax.nn.sigmoid(a)
            hidden[r, c] = (a * gate).astype(BF)
            back = dot_t(gin[r, :], wback[c, :])
            act[r, c] = (back * gate * (1.0 + a * (1.0 - gate))).astype(BF)

        @pl.loop(0, width // 256)
        def _(n):
            c = rows_of(n, 256)
            ing_out[r, c] = dot_t(act[r, :], win[c, :]).astype(BF)

        for c in range(4):
            j = 4 * i + c

            @pl.when(j > 0)
            def _():
                r_copy(j).start()

        @pl.when(i == 0)
        def _():
            own_ing.start()

        xt[:, r] = xin[r, :].T

        @pl.loop(0, width // 256)
        def _(n):
            c = rows_of(n, 256)
            xin[r, c] = dot(hidden[r, :], wback[:, c]).astype(BF)

        for c in range(4):
            ffn_copy(4 * i + c).start()

    tiles = ff // 256

    def sends(t):
        s = t % 4
        to = dict(device_id={"dp": other}, device_id_type=MESH)
        return (
            pltpu.make_async_remote_copy(own_in.at[s], got_in.at[t], t_send.at[0, t], t_recv.at[0, t], **to),
            pltpu.make_async_remote_copy(own_back.at[s], got_back.at[t], t_send.at[1, t], t_recv.at[1, t], **to),
        )

    def writes(t):
        s, c = t % 4, rows_of(t, 256)
        return (
            pltpu.make_async_copy(own_in.at[s], wing_ref.at[:, c], o_sem.at[0, s]),
            pltpu.make_async_copy(own_back.at[s], wbg_ref.at[c, :], o_sem.at[1, s]),
        )

    @pl.loop(0, tiles + 2)
    def _(t):
        @pl.when(t < tiles)
        def _():
            s, c = t % 4, rows_of(t, 256)

            @pl.when(t >= 4)
            def _():
                for copy in writes(t - 4):
                    copy.wait()

            own_in[s] = dot(xt[...], act[:, c]).astype(BF)
            own_back[s] = tdot(hidden[:, c], gin[...]).astype(BF)
            for copy in sends(t):
                copy.start()

        @pl.when(t >= 2)
        def _():
            u = t - 2
            for copy in sends(u):
                copy.wait()
            s = u % 4
            own_in[s] = (own_in[s].astype(F32) + got_in[u].astype(F32)).astype(BF)
            own_back[s] = (own_back[s].astype(F32) + got_back[u].astype(F32)).astype(BF)
            for copy in writes(u):
                copy.start()

    for u in range(tiles - 4, tiles):
        for copy in writes(u):
            copy.wait()
    own_ing.wait()

    @pl.loop(0, experts)
    def _(j):
        ffn_copy(j).wait()

    @pl.loop(1, experts)
    def _(j):
        x_copy(j).wait_send()
        r_copy(j).wait()


def experts_call(experts, capacity, x_slots, g_slots, w_in, w_back):
    total, width = x_slots.shape
    ff = w_in.shape[1]
    tiles = ff // 256
    dma = pltpu.SemaphoreType.DMA
    return pl.pallas_call(
        functools.partial(expert_kernel, experts, capacity),
        out_shape=(
            sds((total, width), BF), sds((total, width), BF), sds((width, ff), BF), sds((ff, width), BF),
        ),
        in_specs=[ANY] * 4,
        out_specs=(ANY,) * 4,
        scratch_shapes=[
            pltpu.VMEM((total, width), BF),
            pltpu.VMEM((total, width), BF),
            pltpu.VMEM((width, ff), BF),
            pltpu.VMEM((ff, width), BF),
            pltpu.VMEM((total, ff), BF),
            pltpu.VMEM((total, ff), BF),
            pltpu.VMEM((total, width), BF),
            pltpu.VMEM((width, total), BF),
            pltpu.VMEM((4, width, 256), BF),
            pltpu.VMEM((4, 256, width), BF),
            pltpu.VMEM((tiles, width, 256), BF),
            pltpu.VMEM((tiles, 256, width), BF),
            dma((experts,)), dma((experts,)), dma((experts,)), dma((experts,)),
            dma((experts,)), dma((2,)), dma((2,)), dma((experts,)),
            dma((2, tiles)), dma((2, tiles)), dma((2, 4)),
        ],
        compiler_params=params(61, collective_id=1, has_side_effects=True),
        cost_estimate=pl.CostEstimate(flops=44 * 10**9, bytes_accessed=30 * 10**6, transcendentals=0),
        name="experts",
    )(x_slots, g_slots, w_in, w_back)


def backward_kernel(
    len_ref, tok_ref, cot_ref, normed_ref, qkv_ref, mixed_ref, laug_ref, h_ref, ret_ref, slot_col_ref,
    wqkv_ref, wout_ref, g1_ref, g2_ref,
    tokg_ref, wqkvg_ref, woutg_ref, g1g_ref, g2g_ref,
    hgrad_ref, hg_ref, mg_ref, daug_ref, kaug_ref, dq_ref, qg_ref, normt_ref,
):
    seq, width = tok_ref.shape
    blocks, pairs = seq // ROWS, width // LANES
    g1g_ref[...] = jnp.zeros_like(g1g_ref)
    g2g_ref[...] = jnp.zeros_like(g2g_ref)
    first = lane_iota((1, LANES)) < HEAD

    @pl.loop(0, blocks)
    def _(i):
        r = rows_of(i)
        hat, inverse = normalize(h_ref[r, :])
        ing = collect(slot_col_ref, ret_ref, r)
        g2g_ref[...] += jnp.sum(ing * hat, axis=0, keepdims=True)
        grad = cot_ref[r, :].astype(F32) + norm_back(ing * g2_ref[...], hat, inverse)
        hgrad_ref[r, :] = grad
        low = grad.astype(BF)
        hg_ref[r, :] = low
        mg = dot_t(low, wout_ref[...]).astype(BF)
        for p in range(pairs):
            part = mg[:, p * LANES : (p + 1) * LANES]
            mg_ref[p, r, :] = part
            prod = part.astype(F32) * mixed_ref[r, p * LANES : (p + 1) * LANES].astype(F32)
            zero = jnp.zeros_like(prod)
            d0 = jnp.sum(jnp.where(first, prod, zero), axis=1, keepdims=True)
            d1 = jnp.sum(jnp.where(first, zero, prod), axis=1, keepdims=True)
            daug_ref[p, r, :] = aug_of(jnp.where(first, d1, d0), 0.0)
        normt_ref[:, r] = normed_ref[r, :].T

    woutg_ref[...] = tdot(mixed_ref[...], hg_ref[...]).astype(BF)
    kaug_ref[...] = key_aug(seq, len_ref[0])
    scale = jnp.asarray(HEAD**-0.5, BF)

    @pl.loop(0, pairs)
    def _(p):
        keep = lane_iota((ROWS, ROWS)) >= lax.broadcasted_iota(I32, (ROWS, ROWS), 0)
        vaug = jnp.where(lane_iota((ROWS, LANES)) % HEAD < 3, 1.0, 0.0).astype(BF)
        none = jnp.zeros((ROWS, LANES), BF)
        dq_ref[...] = jnp.zeros_like(dq_ref)
        for j in range(blocks):
            kr = slice(j * ROWS, (j + 1) * ROWS)
            qr = slice(j * ROWS, seq)
            q = qkv_ref[p, qr, :] * scale
            k = qkv_ref[pairs + p, kr, :]
            v = qkv_ref[2 * pairs + p, kr, :]
            do = mg_ref[p, qr, :]
            la, da = laug_ref[p, qr, :], daug_ref[p, qr, :]
            ka = kaug_ref[kr, :]
            dvs, dks, dss, kms = [], [], [], []
            for head in range(2):
                mine = first if head == 0 else ~first
                s = dot_t(jnp.where(mine, k, ka), jnp.where(mine, q, la))
                e = jnp.exp(s)
                start = jnp.where(keep, e[:, :ROWS], 0.0)
                e = jnp.concatenate([start, e[:, ROWS:]], axis=1) if j < blocks - 1 else start
                dp = dot_t(jnp.where(mine, v, vaug), jnp.where(mine, do, da))
                ds = (e * dp).astype(BF)
                dvs.append(dot(e.astype(BF), do))
                dks.append(dot(ds, q))
                dss.append(ds)
                kms.append(jnp.where(mine, k, none))
            qg_ref[kr, rows_of(2 * pairs + p, LANES)] = jnp.where(first, dvs[0], dvs[1]).astype(BF)
            qg_ref[kr, rows_of(pairs + p, LANES)] = jnp.where(first, dks[0], dks[1]).astype(BF)
            dq_ref[qr, :] += tdot(jnp.concatenate(dss, axis=0), jnp.concatenate(kms, axis=0))
        qg_ref[:, rows_of(p, LANES)] = (dq_ref[...] * HEAD**-0.5).astype(BF)

    @pl.loop(0, 3 * pairs // 2)
    def _(j):
        c = rows_of(j, 2 * LANES)
        wqkvg_ref[:, c] = dot(normt_ref[...], qg_ref[:, c]).astype(BF)

    @pl.loop(0, blocks)
    def _(i):
        r = rows_of(i)
        n1 = dot_t(qg_ref[r, :], wqkv_ref[...])
        hat, inverse = normalize(tok_ref[r, :].astype(F32))
        g1g_ref[...] += jnp.sum(n1 * hat, axis=0, keepdims=True)
        tokg_ref[r, :] = hgrad_ref[r, :] + norm_back(n1 * g1_ref[...], hat, inverse)


def params(mib, **kw):
    return pltpu.CompilerParams(vmem_limit_bytes=mib * MIB, **kw)


def sds(shape, dtype):
    return jax.ShapeDtypeStruct(shape, dtype)


def shards(experts, tokens, lengths, expert_ids, w_qkv, w_out, norm1_gain, norm2_gain, w_in, w_back, cotangent):
    x, g = tokens[0], cotangent[0]
    seq, width = x.shape
    pairs = width // LANES
    capacity = 3 * seq // (2 * experts)
    capacity = (capacity + 15) // 16 * 16
    total = experts * capacity
    eid_row = expert_ids.reshape(1, seq)
    eid_col = expert_ids[0]
    g1, g2 = norm1_gain.reshape(1, width), norm2_gain.reshape(1, width)

    g_slots, _ = pl.pallas_call(
        functools.partial(place_kernel, experts, capacity),
        out_shape=(sds((total, width), BF), sds((1, seq), I32)),
        in_specs=[SMEM, VMEM, VMEM],
        out_specs=(VMEM, VMEM),
        compiler_params=params(40),
        name="place_gradient",
    )(lengths, eid_row, g)
    g_in = exchange(g_slots, experts)

    normed, qkv, mixed, laug, h, x_slots, slot_col = pl.pallas_call(
        functools.partial(forward_kernel, experts, capacity),
        out_shape=(
            sds((seq, width), BF),
            sds((3 * pairs, seq, LANES), BF),
            sds((seq, width), BF),
            sds((pairs, seq, LANES), BF),
            sds((seq, width), F32),
            sds((total, width), BF),
            sds((seq, 1), I32),
        ),
        in_specs=[SMEM] + [VMEM] * 7,
        out_specs=(VMEM,) * 7,
        scratch_shapes=[
            pltpu.VMEM((seq, LANES), BF),
            pltpu.VMEM((seq, width), BF),
            pltpu.VMEM((1, seq), I32),
        ],
        compiler_params=params(58),
        cost_estimate=pl.CostEstimate(flops=40 * 10**9, bytes_accessed=24 * 10**6, transcendentals=0),
        name="attention_forward",
    )(lengths, x, eid_row, eid_col, w_qkv, w_out, g1, g2)
    ing_ret, ffn, wing, wbg = experts_call(experts, capacity, x_slots, g_in, w_in[0], w_back[0])
    ffn_ret = exchange(ffn, experts)

    tokg, wqkvg, woutg, g1g, g2g = pl.pallas_call(
        backward_kernel,
        out_shape=(
            sds((seq, width), F32),
            sds((width, 3 * width), BF),
            sds((width, width), BF),
            sds((1, width), F32),
            sds((1, width), F32),
        ),
        in_specs=[SMEM] + [VMEM] * 13,
        out_specs=(VMEM,) * 5,
        scratch_shapes=[
            pltpu.VMEM((seq, width), F32),
            pltpu.VMEM((seq, width), BF),
            pltpu.VMEM((pairs, seq, LANES), BF),
            pltpu.VMEM((pairs, seq, LANES), BF),
            pltpu.VMEM((seq, LANES), BF),
            pltpu.VMEM((seq, LANES), F32),
            pltpu.VMEM((seq, 3 * width), BF),
            pltpu.VMEM((width, seq), BF),
        ],
        compiler_params=params(60),
        cost_estimate=pl.CostEstimate(flops=60 * 10**9, bytes_accessed=24 * 10**6, transcendentals=0),
        name="attention_backward",
    )(lengths, x, g, normed, qkv, mixed, laug, h, ing_ret, slot_col, w_qkv, w_out, g1, g2)

    output = pl.pallas_call(
        collect_kernel,
        out_shape=sds((seq, width), F32),
        in_specs=[VMEM] * 3,
        out_specs=VMEM,
        compiler_params=params(40),
        name="collect_output",
    )(h, slot_col, ffn_ret)

    in_sum = wing.astype(F32)
    back_sum = wbg.astype(F32)
    both = ("dp", "expert")
    out_sum = lax.psum(woutg, both).astype(F32)
    qkv_sum = lax.psum(wqkvg, both).astype(F32)
    g1_sum, g2_sum = lax.psum((g1g[0], g2g[0]), both)
    return (
        output[None], tokg[None], qkv_sum, out_sum, g1_sum, g2_sum, in_sum[None], back_sum[None],
    )


def exchange(rows, experts):
    total, width = rows.shape
    rows = rows.reshape(experts, total // experts, width)
    return lax.all_to_all(rows, "expert", split_axis=0, concat_axis=0, tiled=True).reshape(total, width)


def solution(mesh):
    split = P(("dp", "expert"), None, None)
    mine = P("expert", None, None)
    return jax.shard_map(
        functools.partial(shards, mesh.shape["expert"]),
        mesh=mesh,
        in_specs=(split, P(("dp", "expert")), split, P(), P(), P(), P(), mine, mine, split),
        out_specs=(split, split, P(), P(), P(), P(), mine, mine),
        check_vma=False,
    )
```

```python
import functools

import jax
import jax.numpy as jnp
from jax import lax
from jax.experimental import pallas as pl
from jax.experimental.pallas import tpu as pltpu
from jax.sharding import PartitionSpec as P

BF, F32, I32 = jnp.bfloat16, jnp.float32, jnp.int32
HEAD = 64
LANES = 128
ROWS = 256
EPS = 1e-5
LAGS = ((0, 1, 3, 4, 5, 7, 8), (0, 1, 3, 4, 5, 7, 8), (0, 1, 3, 4, 5, 6, 7), (0, 1, 2, 3, 4, 5, 6), (0, 1, 2, 3, 4, 5, 6))
NEG = -1e30
VMEM = pl.BlockSpec(memory_space=pltpu.VMEM)
ANY = pl.BlockSpec(memory_space=pl.ANY)
MESH = pl.DeviceIdType.MESH
SMEM = pl.BlockSpec(memory_space=pltpu.SMEM)
MIB = 2**20


def dot(a, b):
    return lax.dot_general(a, b, (((1,), (0,)), ((), ())), preferred_element_type=F32)


def dot_t(a, b):
    return lax.dot_general(a, b, (((1,), (1,)), ((), ())), preferred_element_type=F32)


def tdot(a, b):
    return lax.dot_general(a, b, (((0,), (0,)), ((), ())), preferred_element_type=F32)


def rows_of(i, n=ROWS):
    return pl.ds(pl.multiple_of(i * n, n), n)


def normalize(x):
    center = x - jnp.mean(x, axis=-1, keepdims=True)
    inverse = lax.rsqrt(jnp.mean(center * center, axis=-1, keepdims=True) + EPS)
    return center * inverse, inverse


def norm_back(u, hat, inverse):
    return inverse * (
        u - jnp.mean(u, axis=-1, keepdims=True) - hat * jnp.mean(u * hat, axis=-1, keepdims=True)
    )


def lane_iota(shape):
    return lax.broadcasted_iota(I32, shape, len(shape) - 1)


def split_parts(x):
    high = x.astype(BF)
    rest = x - high.astype(F32)
    middle = rest.astype(BF)
    low = (rest - middle.astype(F32)).astype(BF)
    return high, middle, low


def aug_of(x, one):
    high, middle, low = split_parts(x)
    lane = lane_iota(x.shape) % HEAD
    parts = jnp.where(
        lane == 0,
        -high.astype(F32),
        jnp.where(
            lane == 1,
            -middle.astype(F32),
            jnp.where(lane == 2, -low.astype(F32), jnp.where(lane == 3, one, 0.0)),
        ),
    )
    return parts.astype(BF)


def key_aug(seq, length):
    lane = lane_iota((seq, LANES)) % HEAD
    row = lax.broadcasted_iota(I32, (seq, LANES), 0)
    dead = jnp.where(row < length, 0.0, NEG)
    return jnp.where(lane < 3, 1.0, jnp.where(lane == 3, dead, 0.0)).astype(BF)


def forward_kernel(
    experts, capacity,
    len_ref, eid_row_ref, eid_col_ref, g1_ref, g2_ref, tok_hbm, cot_hbm, wqkv_hbm, wout_hbm,
    normed_out, qkv_out, mixed_out, laug_out, h_out, slots_out, slot_col_ref, g_got,
    tok_ref, cot_ref, wqkv_ref, wout_ref, normed_ref, qkv_ref, mixed_ref, laug_ref, h_ref, slots_ref,
    kaug_ref, xin_ref, slot_row_ref, gs_ref,
    load_sem, store_sem, own_sem, g_send, g_recv,
):
    seq, width = tok_ref.shape
    blocks, pairs = seq // ROWS, width // LANES
    total = experts * capacity
    groups, chunk = experts // 4, 4 * capacity
    length = len_ref[0]
    me = lax.axis_index("expert")

    def block(j):
        return pl.ds(pl.multiple_of(j * capacity, 16), capacity)

    def g_copy(j):
        peer = flip(me, j, experts)
        return pltpu.make_async_remote_copy(
            src_ref=gs_ref.at[block(peer)], dst_ref=g_got.at[block(j)],
            send_sem=g_send.at[j], recv_sem=g_recv.at[j],
            device_id={"expert": peer}, device_id_type=MESH,
        )

    own_g = pltpu.make_async_copy(gs_ref.at[block(me)], g_got.at[block(0)], own_sem)
    loads = [
        pltpu.make_async_copy(src, dst, load_sem.at[i])
        for i, (src, dst) in enumerate(
            ((cot_hbm, cot_ref), (tok_hbm, tok_ref), (wqkv_hbm, wqkv_ref), (wout_hbm, wout_ref))
        )
    ]
    for copy in loads:
        copy.start()
    normed_copy, qkv_copy, mixed_copy, laug_copy, h_copy, slots_copy = [
        pltpu.make_async_copy(src, dst, store_sem.at[i])
        for i, (src, dst) in enumerate(
            (
                (normed_ref, normed_out), (qkv_ref, qkv_out), (mixed_ref, mixed_out), (laug_ref, laug_out),
                (h_ref, h_out), (slots_ref, slots_out),
            )
        )
    ]

    tri = jnp.where(
        lax.broadcasted_iota(I32, (seq, seq), 0) <= lane_iota((seq, seq)), 1.0, 0.0
    ).astype(BF)
    eid = eid_row_ref[...]
    live = lane_iota((1, seq)) < length
    pick = (lax.broadcasted_iota(I32, (experts, seq), 0) == eid) & live
    pick = jnp.where(pick, 1.0, 0.0)
    rank = jnp.sum(dot(pick.astype(BF), tri) * pick, axis=0, keepdims=True).astype(I32) - 1
    slot_row_ref[...] = jnp.where(live, eid * capacity + rank, total)

    greet(experts, False)
    loads[0].wait()

    def send_group(n):
        place(slot_row_ref, cot_ref, gs_ref, flip(me // 4, n, groups), chunk)
        for c in range(4):
            j = 4 * n + c

            @pl.when(j > 0)
            def _():
                g_copy(j).start()

        @pl.when(n == 0)
        def _():
            own_g.start()

    for low, high in ((groups // 2, groups), (0, groups // 2)):

        @pl.loop(low, high)
        def _(n):
            send_group(n)

    for copy in loads[1:]:
        copy.wait()

    @pl.loop(0, blocks)
    def _(i):
        hat, _ = normalize(tok_ref[rows_of(i), :].astype(F32))
        normed_ref[rows_of(i), :] = (hat * g1_ref[...]).astype(BF)

    @pl.loop(0, 3 * pairs // 2)
    def _(j):
        w = wqkv_ref[:, rows_of(j, 2 * LANES)]
        for i in range(blocks):
            r = slice(i * ROWS, (i + 1) * ROWS)
            out = dot(normed_ref[r, :], w).astype(BF)
            qkv_ref[2 * j, r, :] = out[:, :LANES]
            qkv_ref[2 * j + 1, r, :] = out[:, LANES:]

    normed_copy.start()
    qkv_copy.start()
    kaug_ref[...] = key_aug(seq, length)
    first = lane_iota((1, LANES)) < HEAD
    scale = jnp.asarray(HEAD**-0.5, BF)

    @pl.loop(0, pairs)
    def _(p):
        qaug = jnp.where(lane_iota((ROWS, LANES)) % HEAD == 3, 1.0, 0.0).astype(BF)
        causal = lane_iota((ROWS, ROWS)) <= lax.broadcasted_iota(I32, (ROWS, ROWS), 0)
        one = jnp.ones((1, LANES), BF)
        for i in range(blocks):
            r = slice(i * ROWS, (i + 1) * ROWS)
            n = (i + 1) * ROWS
            q = qkv_ref[p, r, :] * scale
            k = qkv_ref[pairs + p, :n, :]
            v = qkv_ref[2 * pairs + p, :n, :]
            aug = kaug_ref[:n, :]
            outs, tops = [], []
            for head in range(2):
                mine = first if head == 0 else ~first
                s = dot_t(jnp.where(mine, q, qaug), jnp.where(mine, k, aug))
                last = jnp.where(causal, s[:, n - ROWS :], NEG)
                s = jnp.concatenate([s[:, : n - ROWS], last], axis=1) if i else last
                top = jnp.max(s, axis=1, keepdims=True)
                e = jnp.exp(s - top).astype(BF)
                outs.append(dot(e, jnp.where(mine, v, one)))
                tops.append(top)
            above = jnp.where(first, outs[0], outs[1])
            below = jnp.where(first, outs[1], outs[0])
            mixed_ref[r, rows_of(p, LANES)] = (above / pltpu.roll(below, HEAD, 1)).astype(BF)
            lse = jnp.where(first, tops[1], tops[0]) + jnp.log(below)
            laug_ref[p, r, :] = aug_of(lse, 1.0)

    mixed_copy.start()
    laug_copy.start()

    @pl.loop(0, blocks)
    def _(i):
        r = rows_of(i)
        h = tok_ref[r, :].astype(F32) + dot(mixed_ref[r, :], wout_ref[...])
        h_ref[r, :] = h
        hat, _ = normalize(h)
        xin_ref[r, :] = (hat * g2_ref[...]).astype(BF)

    h_copy.start()

    @pl.loop(0, groups)
    def _(n):
        place(slot_row_ref, xin_ref, slots_ref, n, chunk)

    slots_copy.start()
    eid = eid_col_ref[...]
    live = lax.broadcasted_iota(I32, (seq, 1), 0) < length
    pick = (lane_iota((seq, LANES)) == eid) & live
    pick = jnp.where(pick, 1.0, 0.0)
    rank = jnp.sum(tdot(tri, pick.astype(BF)) * pick, axis=1, keepdims=True).astype(I32) - 1
    slot_col_ref[...] = jnp.where(live, eid * capacity + rank, experts * capacity)

    own_g.wait()
    for copy in (normed_copy, qkv_copy, mixed_copy, laug_copy, h_copy, slots_copy):
        copy.wait()

    @pl.loop(1, experts)
    def _(j):
        g_copy(j).wait()


def place(slot_row_ref, src_ref, slots_ref, c, step):
    seq = src_ref.shape[0]
    index = lax.broadcasted_iota(I32, (step, seq), 0) + c * step
    onehot = jnp.where(index == slot_row_ref[...], 1.0, 0.0).astype(BF)
    slots_ref[rows_of(c, step), :] = dot(onehot, src_ref[...]).astype(BF)


def collect(slot_col_ref, ret_ref, r):
    total = ret_ref.shape[0]
    onehot = jnp.where(slot_col_ref[r, :] == lane_iota((ROWS, total)), 1.0, 0.0).astype(BF)
    return dot(onehot, ret_ref[...])


def flip(v, j, size):
    out, bit = 0, 1
    while bit < size:
        out = out + bit * ((v // bit + j // bit) % 2)
        bit *= 2
    return out


def greet(experts, with_partner):
    me = lax.axis_index("expert")
    barrier = pltpu.get_barrier_semaphore()

    @pl.loop(1, experts)
    def _(j):
        pl.semaphore_signal(
            barrier, inc=1, device_id={"expert": flip(me, j, experts)}, device_id_type=MESH
        )

    if with_partner:
        pl.semaphore_signal(
            barrier, inc=1, device_id={"dp": 1 - lax.axis_index("dp")}, device_id_type=MESH
        )
    pl.semaphore_wait(barrier, experts - 1 + int(with_partner))


def expert_kernel(
    experts, capacity,
    x_ref, g_ref, win_hbm, wback_hbm,
    ing_ref, ffn_ref, ffn_got, wing_ref, wbg_ref,
    xin, gin, win, wback, hidden, act, ing_out, xt, own_in, own_back, got_in, got_back,
    x_send, x_recv, r_send, r_recv, f_send, f_recv, g_sem, w_sem, own_sem, ffn_sem, t_send, t_recv, o_sem,
):
    me = lax.axis_index("expert")
    other = 1 - lax.axis_index("dp")
    width, ff = win.shape
    groups, chunk = experts // 4, 4 * capacity

    def block(j):
        return pl.ds(pl.multiple_of(j * capacity, 16), capacity)

    def x_copy(j):
        peer = flip(me, j, experts)
        return pltpu.make_async_remote_copy(
            src_ref=x_ref.at[block(peer)], dst_ref=xin.at[block(j)],
            send_sem=x_send.at[j], recv_sem=x_recv.at[j],
            device_id={"expert": peer}, device_id_type=MESH,
        )

    def r_copy(j):
        return pltpu.make_async_remote_copy(
            src_ref=ing_out.at[block(j)], dst_ref=ing_ref.at[block(me)],
            send_sem=r_send.at[j], recv_sem=r_recv.at[j],
            device_id={"expert": flip(me, j, experts)}, device_id_type=MESH,
        )

    load_g = pltpu.make_async_copy(g_ref, gin, g_sem)

    own_x = pltpu.make_async_copy(x_ref.at[block(me)], xin.at[block(0)], own_sem.at[0])
    own_ing = pltpu.make_async_copy(ing_out.at[block(0)], ing_ref.at[block(me)], own_sem.at[1])
    load_in = pltpu.make_async_copy(win_hbm, win, w_sem.at[0])
    load_back = pltpu.make_async_copy(wback_hbm, wback, w_sem.at[1])
    own_x.start()
    load_in.start()
    load_back.start()

    load_g.start()

    greet(experts, True)
    for low, high in ((2, 3), (0, 2), (3, 4)):

        @pl.loop(max(1, experts * low // 4), experts * high // 4)
        def _(j):
            x_copy(j).start()

    own_x.wait()
    load_in.wait()
    load_back.wait()

    load_g.wait()

    def ffn_copy(j):
        peer = flip(me, j, experts)
        return pltpu.make_async_copy(xin.at[block(j)], ffn_ref.at[block(peer)], ffn_sem.at[j])

    def ffn_near(j):
        return pltpu.make_async_remote_copy(
            src_ref=xin.at[block(j)], dst_ref=ffn_got.at[block(me)],
            send_sem=f_send.at[j], recv_sem=f_recv.at[j],
            device_id={"expert": flip(me, j, experts)}, device_id_type=MESH,
        )

    own_ffn = pltpu.make_async_copy(xin.at[block(0)], ffn_got.at[block(me)], own_sem.at[0])

    @pl.loop(0, groups)
    def _(i):
        r = rows_of(i, chunk)
        for c in range(4):
            j = 4 * i + c

            @pl.when(j > 0)
            def _():
                x_copy(j).wait_recv()

        @pl.loop(0, ff // 512)
        def _(t):
            c = rows_of(t, 512)
            a = dot(xin[r, :], win[:, c])
            gate = jax.nn.sigmoid(a)
            hidden[r, c] = (a * gate).astype(BF)
            back = dot_t(gin[r, :], wback[c, :])
            act[r, c] = (back * gate * (1.0 + a * (1.0 - gate))).astype(BF)

        @pl.loop(0, width // 256)
        def _(n):
            c = rows_of(n, 256)
            ing_out[r, c] = dot_t(act[r, :], win[c, :]).astype(BF)

        for c in range(4):
            j = 4 * i + c

            @pl.when(j > 0)
            def _():
                r_copy(j).start()

        @pl.when(i == 0)
        def _():
            own_ing.start()

        xt[:, r] = xin[r, :].T

        @pl.loop(0, width // 256)
        def _(n):
            c = rows_of(n, 256)
            xin[r, c] = dot(hidden[r, :], wback[:, c]).astype(BF)

        for c in range(4):
            j = 4 * i + c

            @pl.when(j >= experts // 2)
            def _():
                ffn_copy(j).start()

            @pl.when((j > 0) & (j < experts // 2))
            def _():
                ffn_near(j).start()

        @pl.when(i == 0)
        def _():
            own_ffn.start()

    tiles = ff // 256

    def sends(t):
        s = t % 4
        to = dict(device_id={"dp": other}, device_id_type=MESH)
        return (
            pltpu.make_async_remote_copy(own_in.at[s], got_in.at[t], t_send.at[0, t], t_recv.at[0, t], **to),
            pltpu.make_async_remote_copy(own_back.at[s], got_back.at[t], t_send.at[1, t], t_recv.at[1, t], **to),
        )

    def writes(t):
        s, c = t % 4, rows_of(t, 256)
        return (
            pltpu.make_async_copy(own_in.at[s], wing_ref.at[:, c], o_sem.at[0, s]),
            pltpu.make_async_copy(own_back.at[s], wbg_ref.at[c, :], o_sem.at[1, s]),
        )

    @pl.loop(0, tiles + 2)
    def _(t):
        @pl.when(t < tiles)
        def _():
            s, c = t % 4, rows_of(t, 256)

            @pl.when(t >= 4)
            def _():
                for copy in writes(t - 4):
                    copy.wait()

            own_in[s] = dot(xt[...], act[:, c]).astype(BF)
            own_back[s] = tdot(hidden[:, c], gin[...]).astype(BF)
            for copy in sends(t):
                copy.start()

        @pl.when(t >= 2)
        def _():
            u = t - 2
            for copy in sends(u):
                copy.wait()
            s = u % 4
            own_in[s] = (own_in[s].astype(F32) + got_in[u].astype(F32)).astype(BF)
            own_back[s] = (own_back[s].astype(F32) + got_back[u].astype(F32)).astype(BF)
            for copy in writes(u):
                copy.start()

    for u in range(tiles - 4, tiles):
        for copy in writes(u):
            copy.wait()
    own_ing.wait()

    own_ffn.wait()

    @pl.loop(experts // 2, experts)
    def _(j):
        ffn_copy(j).wait()

    @pl.loop(1, experts // 2)
    def _(j):
        ffn_near(j).wait()

    @pl.loop(1, experts)
    def _(j):
        x_copy(j).wait_send()
        r_copy(j).wait()


def forward_call(experts, capacity, lengths, eid_row, eid_col, g1, g2, x, g, w_qkv, w_out):
    seq, width = x.shape
    pairs, total = width // LANES, experts * capacity
    dma = pltpu.SemaphoreType.DMA
    vmem = pltpu.VMEM
    return pl.pallas_call(
        functools.partial(forward_kernel, experts, capacity),
        out_shape=(
            sds((seq, width), BF),
            sds((3 * pairs, seq, LANES), BF),
            sds((seq, width), BF),
            sds((pairs, seq, LANES), BF),
            sds((seq, width), F32),
            sds((total, width), BF),
            sds((seq, 1), I32),
            sds((total, width), BF),
        ),
        in_specs=[SMEM] + [VMEM] * 4 + [ANY] * 4,
        out_specs=(ANY,) * 6 + (VMEM, ANY),
        scratch_shapes=[
            vmem((seq, width), BF),
            vmem((seq, width), BF),
            vmem((width, 3 * width), BF),
            vmem((width, width), BF),
            vmem((seq, width), BF),
            vmem((3 * pairs, seq, LANES), BF),
            vmem((seq, width), BF),
            vmem((pairs, seq, LANES), BF),
            vmem((seq, width), F32),
            vmem((total, width), BF),
            vmem((seq, LANES), BF),
            vmem((seq, width), BF),
            vmem((1, seq), I32),
            vmem((total, width), BF),
            dma((4,)), dma((6,)), dma, dma((experts,)), dma((experts,)),
        ],
        compiler_params=params(60, collective_id=4, has_side_effects=True),
        cost_estimate=pl.CostEstimate(flops=40 * 10**9, bytes_accessed=24 * 10**6, transcendentals=0),
        name="attention_forward",
    )(lengths, eid_row, eid_col, g1, g2, x, g, w_qkv, w_out)


def experts_call(experts, capacity, x_slots, g_slots, w_in, w_back):
    total, width = x_slots.shape
    ff = w_in.shape[1]
    tiles = ff // 256
    dma = pltpu.SemaphoreType.DMA
    return pl.pallas_call(
        functools.partial(expert_kernel, experts, capacity),
        out_shape=(
            sds((total, width), BF), sds((total, width), BF), sds((total, width), BF),
            sds((width, ff), BF), sds((ff, width), BF),
        ),
        in_specs=[ANY] * 4,
        out_specs=(ANY,) * 5,
        scratch_shapes=[
            pltpu.VMEM((total, width), BF),
            pltpu.VMEM((total, width), BF),
            pltpu.VMEM((width, ff), BF),
            pltpu.VMEM((ff, width), BF),
            pltpu.VMEM((total, ff), BF),
            pltpu.VMEM((total, ff), BF),
            pltpu.VMEM((total, width), BF),
            pltpu.VMEM((width, total), BF),
            pltpu.VMEM((4, width, 256), BF),
            pltpu.VMEM((4, 256, width), BF),
            pltpu.VMEM((tiles, width, 256), BF),
            pltpu.VMEM((tiles, 256, width), BF),
            dma((experts,)), dma((experts,)), dma((experts,)), dma((experts,)),
            dma((experts // 2,)), dma((experts // 2,)),
            dma, dma((2,)), dma((2,)), dma((experts,)),
            dma((2, tiles)), dma((2, tiles)), dma((2, 4)),
        ],
        compiler_params=params(61, collective_id=1, has_side_effects=True),
        cost_estimate=pl.CostEstimate(flops=44 * 10**9, bytes_accessed=30 * 10**6, transcendentals=0),
        name="experts",
    )(x_slots, g_slots, w_in, w_back)


def unit_plan(experts, width):
    pairs = width // LANES
    runs = [None] + [(p, p + 1) for p in range(0, pairs - 2, 2)] + [(p,) for p in range(pairs - pairs % 2 - 2, pairs)]
    plan, row = [], 0
    for run in runs:
        tiles = pairs if run is None else 3 * len(run)
        piece = -(-tiles * width // (2 * experts * 16)) * 16
        plan.append((row, run, piece))
        row += 2 * experts * piece
    return plan, row


def backward_kernel(
    experts, capacity,
    len_ref, g1_ref, g2_ref, tok_hbm, cot_hbm, normed_hbm, qkv_hbm, mixed_hbm, laug_hbm, h_hbm, ret_hbm, slot_col_ref,
    wqkv_hbm, wout_hbm, ffn_hbm, got_hbm,
    out_ref, tokg_ref, sums_ref, g2g_ref,
    tok_ref, qkv_ref, mixed_ref, laug_ref, h_ref, ret_ref, wqkv_ref, wout_ref, ffn_ref,
    hgrad_ref, hg_ref, mg_ref, daug_ref, kaug_ref, dq_ref, qg_ref, normt_ref,
    part, final, got_core, got_in, got_out, g2_acc,
    load_sem, f_send, f_recv, core_send, core_recv, in_send, in_recv, out_send, out_recv, o_sem,
):
    seq, width = tok_ref.shape
    blocks, pairs, total = seq // ROWS, width // LANES, experts * capacity
    me, core = lax.axis_index("expert"), lax.axis_index("dp")
    inner = 2 ** ((experts.bit_length() - 1) // 2)
    outer = experts // inner

    def bits_of(u):
        bits = list(range(experts.bit_length() - 1))
        turn = u % (len(bits) - 1)
        order = bits[turn:-1] + bits[:turn] + bits[-1:]
        return order[: len(bits) // 2], order[len(bits) // 2 :]

    def place_in(bits):
        return sum(me // 2**b % 2 * 2**k for k, b in enumerate(bits))

    def peer_in(bits, i):
        return flip(me, sum(i // 2**k % 2 * 2**b for k, b in enumerate(bits)), experts)

    def places(u):
        return [place_in(bits) for bits in bits_of(u)]

    plan, _ = unit_plan(experts, width)
    first = lane_iota((1, LANES)) < HEAD

    def block(j):
        return pl.ds(pl.multiple_of(j * capacity, 16), capacity)

    def rows(start, size):
        return pl.ds(pl.multiple_of(start, 16), size)

    def ffn_copy(j):
        peer = flip(me, j, experts)
        return pltpu.make_async_remote_copy(
            src_ref=ffn_hbm.at[block(peer)], dst_ref=ffn_ref.at[block(me)],
            send_sem=f_send.at[j], recv_sem=f_recv.at[j],
            device_id={"expert": peer}, device_id_type=MESH,
        )

    close = pl.ds(pl.multiple_of(me // (experts // 2) * total // 2, 16), total // 2)
    near_ffn = pltpu.make_async_copy(got_hbm.at[close], ffn_ref.at[close], load_sem.at[0])
    loads = [
        pltpu.make_async_copy(src, dst, load_sem.at[1 + i])
        for i, (src, dst) in enumerate(
            (
                (ret_hbm, ret_ref),
                (h_hbm, h_ref),
                (cot_hbm, tok_ref),
                (wout_hbm, wout_ref),
                (mixed_hbm, mixed_ref),
                (normed_hbm, qg_ref.at[:, :width]),
                (qkv_hbm, qkv_ref),
                (laug_hbm, laug_ref),
                (wqkv_hbm, wqkv_ref),
            )
        )
    ]
    for copy in loads[:5]:
        copy.start()
    load_tok = pltpu.make_async_copy(tok_hbm, tok_ref, load_sem.at[10])
    greet(experts, True)

    def send_ffn(r):
        share = experts // 16
        for j in range(r * share, (r + 1) * share):
            ffn_copy(experts // 2 + j).start()

    send_ffn(0)
    send_ffn(1)
    near_ffn.start()
    for copy in loads[5:]:
        copy.start()

    def core_copy(u, back):
        start, _, piece = plan[u]
        half = experts * piece
        src = final if back else part
        mine, theirs = start + core * half, start + (1 - core) * half
        return pltpu.make_async_remote_copy(
            src_ref=src.at[rows(mine if back else theirs, half)],
            dst_ref=final.at[rows(mine, half)] if back else got_core.at[rows(start // 2, half)],
            send_sem=core_send.at[u, back], recv_sem=core_recv.at[u, back],
            device_id={"dp": 1 - core}, device_id_type=MESH,
        )

    def inner_copy(u, back, i):
        start, _, piece = plan[u]
        size = outer * piece
        base = start + core * experts * piece
        near = places(u)[0]
        peer = flip(near, i, inner)
        src, dst = (
            (final.at[rows(base + near * size, size)], final.at[rows(base + near * size, size)])
            if back
            else (
                part.at[rows(base + peer * size, size)],
                got_in.at[i - 1, rows(start // (2 * inner), size)],
            )
        )
        return pltpu.make_async_remote_copy(
            src_ref=src, dst_ref=dst,
            send_sem=in_send.at[u, back, i], recv_sem=in_recv.at[u, back, i],
            device_id={"expert": peer_in(bits_of(u)[0], i)}, device_id_type=MESH,
        )

    def outer_copy(u, back, i):
        start, _, piece = plan[u]
        near, far = places(u)
        base = start + core * experts * piece + near * outer * piece
        peer = flip(far, i, outer)
        src, dst = (
            (final.at[rows(base + far * piece, piece)], final.at[rows(base + far * piece, piece)])
            if back
            else (
                part.at[rows(base + peer * piece, piece)],
                got_out.at[i - 1, rows(start // (2 * experts), piece)],
            )
        )
        return pltpu.make_async_remote_copy(
            src_ref=src, dst_ref=dst,
            send_sem=out_send.at[u, back, i], recv_sem=out_recv.at[u, back, i],
            device_id={"expert": peer_in(bits_of(u)[1], i)}, device_id_type=MESH,
        )

    def add_up(to, at, got, count, start, size, dst_at):
        step = 16 * max(k for k in (1, 2, 3, 4, 6, 8, 9, 12) if size // 16 % k == 0)

        @pl.loop(0, size // step)
        def _(n):
            o = n * step
            total = part[rows(at + o, step), :].astype(F32)
            for i in range(count):
                got_at = got.at[rows(start + o, step)] if count == 1 else got.at[i, rows(start + o, step)]
                total = total + got_at[...].astype(F32)
            to[rows(dst_at + o, step), :] = total.astype(BF)

    def advance(u, stage):
        start, _, piece = plan[u]
        base = start + core * experts * piece
        near, far = places(u)
        if stage == 0:
            core_copy(u, 0).start()
        elif stage == 1:
            core_copy(u, 0).wait()
            add_up(part, base, got_core, 1, start // 2, experts * piece, base)
            for i in range(1, inner):
                inner_copy(u, 0, i).start()
        elif stage == 2:
            for i in range(1, inner):
                inner_copy(u, 0, i).wait()
            at = base + near * outer * piece
            add_up(part, at, got_in, inner - 1, start // (2 * inner), outer * piece, at)
            for i in range(1, outer):
                outer_copy(u, 0, i).start()
        elif stage == 3:
            for i in range(1, outer):
                outer_copy(u, 0, i).wait()
            at = base + (near * outer + far) * piece
            add_up(final, at, got_out, outer - 1, start // (2 * experts), piece, at)
            for i in range(1, outer):
                outer_copy(u, 1, i).start()
        elif stage == 4:
            for i in range(1, outer):
                outer_copy(u, 1, i).wait()
            for i in range(1, inner):
                inner_copy(u, 1, i).start()
        elif stage == 5:
            for i in range(1, inner):
                inner_copy(u, 1, i).wait()
            core_copy(u, 1).start()
        else:
            core_copy(u, 1).wait()
            for copy in sums_copies(u):
                copy.start()

    def sums_copies(u):
        start, run, _ = plan[u]
        tiles = [3 * pairs + n for n in range(pairs)] if run is None else [n * pairs + p for p in run for n in range(3)]
        return [
            pltpu.make_async_copy(final.at[start + i * width : start + (i + 1) * width], sums_ref.at[tile], o_sem.at[tile])
            for i, tile in enumerate(tiles)
        ]

    for copy in loads[:5]:
        copy.wait()

    g2_acc[...] = jnp.zeros_like(g2_acc)

    @pl.loop(0, blocks)
    def _(i):
        r = rows_of(i)
        hat, inverse = normalize(h_ref[r, :])
        ing = collect(slot_col_ref, ret_ref, r)
        g2_acc[...] += jnp.sum((ing * hat).reshape(ROWS // 8, 8, width), axis=0)
        grad = tok_ref[r, :].astype(F32) + norm_back(ing * g2_ref[...], hat, inverse)
        hgrad_ref[r, :] = grad
        low = grad.astype(BF)
        hg_ref[r, :] = low
        mg = dot_t(low, wout_ref[...]).astype(BF)

        @pl.when(i == blocks // 2)
        def _():
            send_ffn(2)

        for p in range(pairs):
            piece = mg[:, p * LANES : (p + 1) * LANES]
            mg_ref[p, r, :] = piece
            prod = piece.astype(F32) * mixed_ref[r, p * LANES : (p + 1) * LANES].astype(F32)
            zero = jnp.zeros_like(prod)
            d0 = jnp.sum(jnp.where(first, prod, zero), axis=1, keepdims=True)
            d1 = jnp.sum(jnp.where(first, zero, prod), axis=1, keepdims=True)
            daug_ref[p, r, :] = aug_of(jnp.where(first, d1, d0), 0.0)

    load_tok.start()

    for u, (start, run, piece) in enumerate(plan):
        tiles = pairs if run is None else 3 * len(run)
        spare = 2 * experts * piece - tiles * width
        if spare:
            part[start + tiles * width : start + tiles * width + spare, :] = jnp.zeros((spare, LANES), BF)
            gain_at = start + tiles * width
    for p in range(pairs):
        gain = jnp.sum(g2_acc[:, p * LANES : (p + 1) * LANES], axis=0, keepdims=True)
        part[gain_at + 16 * p : gain_at + 16 * p + 1, :] = gain.astype(BF)

    @pl.loop(0, width // 256)
    def _(n):
        out = tdot(mixed_ref[...], hg_ref[:, rows_of(n, 256)]).astype(BF)
        at = plan[0][0] + 2 * n * width
        part[rows(at, width), :] = out[:, :LANES]
        part[rows(at + width, width), :] = out[:, LANES:]

    send_ffn(3)
    advance(0, 0)
    loads[5].wait()

    @pl.loop(0, blocks)
    def _(i):
        r = rows_of(i)
        normt_ref[:, r] = qg_ref[r, :width].T

    kaug_ref[...] = key_aug(seq, len_ref[0])
    scale = jnp.asarray(HEAD**-0.5, BF)
    for copy in loads[6:]:
        copy.wait()

    ends = {}
    for u, (_, run, _) in enumerate(plan):
        ready = -1 if run is None else run[-1]
        for stage, late in enumerate(LAGS[u]):
            if ready + late >= 0:
                ends.setdefault(ready + late, []).append((u, stage))

    @pl.loop(0, pairs)
    def _(p):
        keep = lane_iota((ROWS, ROWS)) >= lax.broadcasted_iota(I32, (ROWS, ROWS), 0)
        vaug = jnp.where(lane_iota((ROWS, LANES)) % HEAD < 3, 1.0, 0.0).astype(BF)
        none = jnp.zeros((ROWS, LANES), BF)
        dq_ref[...] = jnp.zeros_like(dq_ref)
        for j in range(blocks):
            kr = slice(j * ROWS, (j + 1) * ROWS)
            qr = slice(j * ROWS, seq)
            q = qkv_ref[p, qr, :] * scale
            k = qkv_ref[pairs + p, kr, :]
            v = qkv_ref[2 * pairs + p, kr, :]
            do = mg_ref[p, qr, :]
            la, da = laug_ref[p, qr, :], daug_ref[p, qr, :]
            ka = kaug_ref[kr, :]
            dvs, dks, dss, kms = [], [], [], []
            for head in range(2):
                mine = first if head == 0 else ~first
                s = dot_t(jnp.where(mine, k, ka), jnp.where(mine, q, la))
                e = jnp.exp(s)
                start = jnp.where(keep, e[:, :ROWS], 0.0)
                e = jnp.concatenate([start, e[:, ROWS:]], axis=1) if j < blocks - 1 else start
                dp = dot_t(jnp.where(mine, v, vaug), jnp.where(mine, do, da))
                ds = (e * dp).astype(BF)
                dvs.append(dot(e.astype(BF), do))
                dks.append(dot(ds, q))
                dss.append(ds)
                kms.append(jnp.where(mine, k, none))
            qg_ref[kr, rows_of(2 * pairs + p, LANES)] = jnp.where(first, dvs[0], dvs[1]).astype(BF)
            qg_ref[kr, rows_of(pairs + p, LANES)] = jnp.where(first, dks[0], dks[1]).astype(BF)
            dq_ref[qr, :] += tdot(jnp.concatenate(dss, axis=0), jnp.concatenate(kms, axis=0))
        qg_ref[:, rows_of(p, LANES)] = (dq_ref[...] * HEAD**-0.5).astype(BF)

        tiles3 = [qg_ref[:, rows_of(n * pairs + p, LANES)] for n in range(3)]
        out = dot(normt_ref[...], jnp.concatenate(tiles3, axis=1)).astype(BF)
        for u, (start, run, _) in enumerate(plan):
            if run is not None:

                @pl.when((p >= run[0]) & (p <= run[-1]))
                def _():
                    for n in range(3):
                        at = start + ((p - run[0]) * 3 + n) * width
                        part[rows(at, width), :] = out[:, n * LANES : (n + 1) * LANES]

        for at in range(pairs):

            @pl.when(p == at)
            def _():
                if at < 4:
                    send_ffn(4 + at)
                for u, stage in ends.get(at, ()):
                    advance(u, stage)

    load_tok.wait()

    def finish_tokens(i):
        r = rows_of(i)
        n1 = dot_t(qg_ref[r, :], wqkv_ref[...])
        hat, inverse = normalize(tok_ref[r, :].astype(F32))
        hgrad_ref[r, :] = hgrad_ref[r, :] + norm_back(n1 * g1_ref[...], hat, inverse)
        tokg_copy(i).start()

    def tokg_copy(i):
        return pltpu.make_async_copy(hgrad_ref.at[rows_of(i)], tokg_ref.at[rows_of(i)], load_sem.at[1 + i])

    def finish_output(i):
        r = rows_of(i)
        h_ref[r, :] = h_ref[r, :] + collect(slot_col_ref, ffn_ref, r)
        out_copy(i).start()

    def out_copy(i):
        return pltpu.make_async_copy(h_ref.at[rows_of(i)], out_ref.at[rows_of(i)], load_sem.at[1 + blocks + i])

    last = max(ends)
    for step in range(pairs, last + 1):
        n = step - pairs
        if n < blocks:
            finish_tokens(n)
        elif n == blocks:
            near_ffn.wait()

            @pl.loop(experts // 2, experts)
            def _(j):
                ffn_copy(j).wait()

            for i in range(blocks // 2):
                finish_output(i)
        elif n == blocks + 1:
            for i in range(blocks // 2, blocks):
                finish_output(i)
        for u, stage in ends.get(step, ()):
            advance(u, stage)

    for p in range(pairs):
        g2g_ref[:, p * LANES : (p + 1) * LANES] = final[gain_at + 16 * p : gain_at + 16 * p + 1, :].astype(F32)
    for i in range(blocks):
        tokg_copy(i).wait()
        out_copy(i).wait()
    for u in range(len(plan)):
        for copy in sums_copies(u):
            copy.wait()


def backward_call(experts, capacity, lengths, g1, g2, x, g, normed, qkv, mixed, laug, h, ret, slot_col, w_qkv, w_out, ffn, got):
    seq, width = x.shape
    pairs, total = width // LANES, experts * capacity
    plan, height = unit_plan(experts, width)
    inner = 2 ** ((experts.bit_length() - 1) // 2)
    outer, units = experts // inner, len(plan)
    dma = pltpu.SemaphoreType.DMA
    vmem = pltpu.VMEM
    return pl.pallas_call(
        functools.partial(backward_kernel, experts, capacity),
        out_shape=(
            sds((seq, width), F32), sds((seq, width), F32), sds((4 * pairs, width, LANES), BF), sds((1, width), F32),
        ),
        in_specs=[SMEM, VMEM, VMEM] + [ANY] * 8 + [VMEM] + [ANY] * 4,
        out_specs=(ANY, ANY, ANY, VMEM),
        scratch_shapes=[
            vmem((seq, width), BF),
            vmem((3 * pairs, seq, LANES), BF),
            vmem((seq, width), BF),
            vmem((pairs, seq, LANES), BF),
            vmem((seq, width), F32),
            vmem((total, width), BF),
            vmem((width, 3 * width), BF),
            vmem((width, width), BF),
            vmem((total, width), BF),
            vmem((seq, width), F32),
            vmem((seq, width), BF),
            vmem((pairs, seq, LANES), BF),
            vmem((pairs, seq, LANES), BF),
            vmem((seq, LANES), BF),
            vmem((seq, LANES), F32),
            vmem((seq, 3 * width), BF),
            vmem((width, seq), BF),
            vmem((height, LANES), BF),
            vmem((height, LANES), BF),
            vmem((height // 2, LANES), BF),
            vmem((inner - 1, height // (2 * inner), LANES), BF),
            vmem((outer - 1, height // (2 * experts), LANES), BF),
            vmem((8, width), F32),
            dma((11,)), dma((experts,)), dma((experts,)),
            dma((units, 2)), dma((units, 2)),
            dma((units, 2, inner)), dma((units, 2, inner)),
            dma((units, 2, outer)), dma((units, 2, outer)),
            dma((4 * pairs,)),
        ],
        compiler_params=params(62, collective_id=2, has_side_effects=True),
        cost_estimate=pl.CostEstimate(flops=60 * 10**9, bytes_accessed=24 * 10**6, transcendentals=0),
        name="attention_backward",
    )(lengths, g1, g2, x, g, normed, qkv, mixed, laug, h, ret, slot_col, w_qkv, w_out, ffn, got)


def finish_kernel(
    win_ref, wback_ref, sums_ref, wqkv_ref, g1_ref,
    win_out, wback_out, wqkv_out, wout_out, g1g_ref,
    gain_ref,
):
    i = pl.program_id(0)
    size = wqkv_ref.shape[0]
    tiles = sums_ref.shape[0]
    pairs = tiles // 4
    win_out[...] = win_ref[...].astype(F32)
    wback_out[...] = wback_ref[...].astype(F32)
    gain = jnp.zeros((size, LANES), F32)
    for t in range(tiles):
        tile = sums_ref[t].astype(F32)
        if t < 3 * pairs:
            c = slice(t * LANES, (t + 1) * LANES)
            wqkv_out[:, c] = tile
            gain = gain + tile * wqkv_ref[:, c].astype(F32)
        else:
            wout_out[:, (t - 3 * pairs) * LANES : (t - 3 * pairs + 1) * LANES] = tile
    gain_ref[rows_of(i, size), :] = gain

    @pl.when(i == pl.num_programs(0) - 1)
    def _():
        total = lax.dot_general(
            jnp.ones((8, LANES), F32), gain_ref[...], (((1,), (1,)), ((), ())),
            precision=lax.Precision.HIGHEST, preferred_element_type=F32,
        )
        g1g_ref[...] = total[:1, :] / g1_ref[...]


def finish_call(win, wback, sums, w_qkv, g1):
    width, ff = win.shape
    tiles, steps = sums.shape[0], 8
    wide = pl.BlockSpec((width // steps, ff), lambda i: (i, 0))
    tall = pl.BlockSpec((ff // steps, width), lambda i: (i, 0))
    three = pl.BlockSpec((width // steps, 3 * width), lambda i: (i, 0))
    square = pl.BlockSpec((width // steps, width), lambda i: (i, 0))
    row = pl.BlockSpec((1, width), lambda i: (0, 0))
    return pl.pallas_call(
        finish_kernel,
        grid=(steps,),
        out_shape=(
            sds((width, ff), F32), sds((ff, width), F32), sds((width, 3 * width), F32), sds((width, width), F32),
            sds((1, width), F32),
        ),
        in_specs=[wide, tall, pl.BlockSpec((tiles, width // steps, LANES), lambda i: (0, i, 0)), three, row],
        out_specs=(wide, tall, three, square, row),
        scratch_shapes=[pltpu.VMEM((width, LANES), F32)],
        compiler_params=params(61),
        name="finish_gradients",
    )(win, wback, sums, w_qkv, g1)


def params(mib, **kw):
    return pltpu.CompilerParams(vmem_limit_bytes=mib * MIB, **kw)


def sds(shape, dtype):
    return jax.ShapeDtypeStruct(shape, dtype)


def shards(experts, tokens, lengths, expert_ids, w_qkv, w_out, norm1_gain, norm2_gain, w_in, w_back, cotangent):
    x, g = tokens[0], cotangent[0]
    seq, width = x.shape
    pairs = width // LANES
    capacity = 3 * seq // (2 * experts)
    capacity = (capacity + 15) // 16 * 16
    total = experts * capacity
    eid_row = expert_ids.reshape(1, seq)
    eid_col = expert_ids[0]
    g1, g2 = norm1_gain.reshape(1, width), norm2_gain.reshape(1, width)

    normed, qkv, mixed, laug, h, x_slots, slot_col, g_in = forward_call(
        experts, capacity, lengths, eid_row, eid_col, g1, g2, x, g, w_qkv, w_out
    )
    ing_ret, ffn, got, wing, wbg = experts_call(experts, capacity, x_slots, g_in, w_in[0], w_back[0])
    output, tokg, sums, g2_sum = backward_call(
        experts, capacity, lengths, g1, g2, x, g, normed, qkv, mixed, laug, h, ing_ret, slot_col, w_qkv, w_out, ffn, got
    )
    in_sum, back_sum, qkv_sum, out_sum, g1_sum = finish_call(wing, wbg, sums, w_qkv, g1)
    return (
        output[None], tokg[None], qkv_sum, out_sum, g1_sum[0], g2_sum[0], in_sum[None], back_sum[None],
    )


def solution(mesh):
    split = P(("dp", "expert"), None, None)
    mine = P("expert", None, None)
    return jax.shard_map(
        functools.partial(shards, mesh.shape["expert"]),
        mesh=mesh,
        in_specs=(split, P(("dp", "expert")), split, P(), P(), P(), P(), mine, mine, split),
        out_specs=(split, split, P(), P(), P(), P(), mine, mine),
        check_vma=False,
    )
```

```python
import functools

import jax
import jax.numpy as jnp
from jax import lax
from jax.experimental import pallas as pl
from jax.experimental.pallas import tpu as pltpu
from jax.sharding import PartitionSpec as P

BF, F32, I32 = jnp.bfloat16, jnp.float32, jnp.int32
HEAD = 64
LANES = 128
ROWS = 256
EPS = 1e-5
INNER = 8
STAGES = ((-1, 0, 1, 2, 4, 5, 6, 7), (0, 1, 2, 3, 5, 6, 7, 8), (1, 2, 3, 4, 6, 7, 8, 9), (2, 3, 4, 5, 6, 7, 8, 9), (3, 4, 5, 6, 7, 8, 9, 10), (4, 5, 6, 7, 8, 9, 10, 11), (5, 6, 7, 8, 9, 10, 11, 12))
NEG = -1e30
VMEM = pl.BlockSpec(memory_space=pltpu.VMEM)
ANY = pl.BlockSpec(memory_space=pl.ANY)
MESH = pl.DeviceIdType.MESH
SMEM = pl.BlockSpec(memory_space=pltpu.SMEM)
MIB = 2**20


def dot(a, b):
    return lax.dot_general(a, b, (((1,), (0,)), ((), ())), preferred_element_type=F32)


def dot_t(a, b):
    return lax.dot_general(a, b, (((1,), (1,)), ((), ())), preferred_element_type=F32)


def tdot(a, b):
    return lax.dot_general(a, b, (((0,), (0,)), ((), ())), preferred_element_type=F32)


def rows_of(i, n=ROWS):
    return pl.ds(pl.multiple_of(i * n, n), n)


def normalize(x):
    center = x - jnp.mean(x, axis=-1, keepdims=True)
    inverse = lax.rsqrt(jnp.mean(center * center, axis=-1, keepdims=True) + EPS)
    return center * inverse, inverse


def norm_back(u, hat, inverse):
    return inverse * (
        u - jnp.mean(u, axis=-1, keepdims=True) - hat * jnp.mean(u * hat, axis=-1, keepdims=True)
    )


def lane_iota(shape):
    return lax.broadcasted_iota(I32, shape, len(shape) - 1)


def split_parts(x):
    high = x.astype(BF)
    rest = x - high.astype(F32)
    middle = rest.astype(BF)
    low = (rest - middle.astype(F32)).astype(BF)
    return high, middle, low


def aug_of(x, one):
    high, middle, low = split_parts(x)
    lane = lane_iota(x.shape) % HEAD
    parts = jnp.where(
        lane == 0,
        -high.astype(F32),
        jnp.where(
            lane == 1,
            -middle.astype(F32),
            jnp.where(lane == 2, -low.astype(F32), jnp.where(lane == 3, one, 0.0)),
        ),
    )
    return parts.astype(BF)


def key_aug(seq, length):
    lane = lane_iota((seq, LANES)) % HEAD
    row = lax.broadcasted_iota(I32, (seq, LANES), 0)
    dead = jnp.where(row < length, 0.0, NEG)
    return jnp.where(lane < 3, 1.0, jnp.where(lane == 3, dead, 0.0)).astype(BF)


def forward_kernel(
    experts, capacity,
    len_ref, eid_row_ref, g1_ref, g2_ref, tok_hbm, cot_hbm, wqkv_hbm, wout_hbm,
    normed_out, qkv_out, mixed_out, laug_out, h_out, slots_out, slot_col_ref, g_got,
    tok_ref, cot_ref, wqkv_ref, wout_ref, normed_ref, qkv_ref, mixed_ref, laug_ref, h_ref, slots_ref,
    kaug_ref, xin_ref, slot_row_ref, gs_ref,
    load_sem, store_sem, own_sem, g_send, g_recv,
):
    seq, width = tok_ref.shape
    blocks, pairs = seq // ROWS, width // LANES
    total = experts * capacity
    groups, chunk = experts // 4, 4 * capacity
    length = len_ref[0]
    me = lax.axis_index("expert")

    def block(j):
        return pl.ds(pl.multiple_of(j * capacity, 16), capacity)

    def g_copy(j):
        peer = flip(me, j, experts)
        return pltpu.make_async_remote_copy(
            src_ref=gs_ref.at[block(peer)], dst_ref=g_got.at[block(j)],
            send_sem=g_send.at[j], recv_sem=g_recv.at[j],
            device_id={"expert": peer}, device_id_type=MESH,
        )

    own_g = pltpu.make_async_copy(gs_ref.at[block(me)], g_got.at[block(0)], own_sem)
    loads = [
        pltpu.make_async_copy(src, dst, load_sem.at[i])
        for i, (src, dst) in enumerate(
            ((cot_hbm, cot_ref), (tok_hbm, tok_ref), (wqkv_hbm, wqkv_ref), (wout_hbm, wout_ref))
        )
    ]
    for copy in loads:
        copy.start()
    normed_copy, qkv_copy, mixed_copy, laug_copy, h_copy, slots_copy = [
        pltpu.make_async_copy(src, dst, store_sem.at[i])
        for i, (src, dst) in enumerate(
            (
                (normed_ref, normed_out), (qkv_ref, qkv_out), (mixed_ref, mixed_out), (laug_ref, laug_out),
                (h_ref, h_out), (slots_ref, slots_out),
            )
        )
    ]

    tri = jnp.where(
        lax.broadcasted_iota(I32, (seq, seq), 0) <= lane_iota((seq, seq)), 1.0, 0.0
    ).astype(BF)
    eid = eid_row_ref[...]
    live = lane_iota((1, seq)) < length
    pick = (lax.broadcasted_iota(I32, (experts, seq), 0) == eid) & live
    pick = jnp.where(pick, 1.0, 0.0)
    rank = jnp.sum(dot(pick.astype(BF), tri) * pick, axis=0, keepdims=True).astype(I32) - 1
    slot_row_ref[...] = jnp.where(live, eid * capacity + rank, total)

    greet(experts, False)
    loads[0].wait()

    def send_group(n):
        place(slot_row_ref, cot_ref, gs_ref, flip(me // 4, n, groups), chunk)
        for c in range(4):
            j = 4 * n + c

            @pl.when(j > 0)
            def _():
                g_copy(j).start()

        @pl.when(n == 0)
        def _():
            own_g.start()

    for low, high in ((groups // 2, groups), (0, groups // 2)):

        @pl.loop(low, high)
        def _(n):
            send_group(n)

    for copy in loads[1:]:
        copy.wait()

    @pl.loop(0, blocks)
    def _(i):
        hat, _ = normalize(tok_ref[rows_of(i), :].astype(F32))
        normed_ref[rows_of(i), :] = (hat * g1_ref[...].reshape(1, width)).astype(BF)

    @pl.loop(0, 3 * pairs // 2)
    def _(j):
        w = wqkv_ref[:, rows_of(j, 2 * LANES)]
        for i in range(blocks):
            r = slice(i * ROWS, (i + 1) * ROWS)
            out = dot(normed_ref[r, :], w).astype(BF)
            qkv_ref[2 * j, r, :] = out[:, :LANES]
            qkv_ref[2 * j + 1, r, :] = out[:, LANES:]

    normed_copy.start()
    qkv_copy.start()
    kaug_ref[...] = key_aug(seq, length)
    first = lane_iota((1, LANES)) < HEAD
    scale = jnp.asarray(HEAD**-0.5, BF)

    @pl.loop(0, pairs)
    def _(p):
        qaug = jnp.where(lane_iota((ROWS, LANES)) % HEAD == 3, 1.0, 0.0).astype(BF)
        causal = lane_iota((ROWS, ROWS)) <= lax.broadcasted_iota(I32, (ROWS, ROWS), 0)
        one = jnp.ones((1, LANES), BF)
        for i in range(blocks):
            r = slice(i * ROWS, (i + 1) * ROWS)
            n = (i + 1) * ROWS
            q = qkv_ref[p, r, :] * scale
            k = qkv_ref[pairs + p, :n, :]
            v = qkv_ref[2 * pairs + p, :n, :]
            aug = kaug_ref[:n, :]
            outs, tops = [], []
            for head in range(2):
                mine = first if head == 0 else ~first
                s = dot_t(jnp.where(mine, q, qaug), jnp.where(mine, k, aug))
                last = jnp.where(causal, s[:, n - ROWS :], NEG)
                s = jnp.concatenate([s[:, : n - ROWS], last], axis=1) if i else last
                top = jnp.max(s, axis=1, keepdims=True)
                e = jnp.exp(s - top).astype(BF)
                outs.append(dot(e, jnp.where(mine, v, one)))
                tops.append(top)
            above = jnp.where(first, outs[0], outs[1])
            below = jnp.where(first, outs[1], outs[0])
            mixed_ref[r, rows_of(p, LANES)] = (above / pltpu.roll(below, HEAD, 1)).astype(BF)
            lse = jnp.where(first, tops[1], tops[0]) + jnp.log(below)
            laug_ref[p, r, :] = aug_of(lse, 1.0)

    mixed_copy.start()
    laug_copy.start()

    @pl.loop(0, blocks)
    def _(i):
        r = rows_of(i)
        h = tok_ref[r, :].astype(F32) + dot(mixed_ref[r, :], wout_ref[...])
        h_ref[r, :] = h
        hat, _ = normalize(h)
        xin_ref[r, :] = (hat * g2_ref[...].reshape(1, width)).astype(BF)

    h_copy.start()

    @pl.loop(0, groups)
    def _(n):
        place(slot_row_ref, xin_ref, slots_ref, n, chunk)

    slots_copy.start()
    eid = jnp.broadcast_to(eid_row_ref[...].astype(F32), (LANES, seq)).T.astype(I32)
    live = lax.broadcasted_iota(I32, (seq, 1), 0) < length
    pick = (lane_iota((seq, LANES)) == eid) & live
    pick = jnp.where(pick, 1.0, 0.0)
    rank = jnp.sum(tdot(tri, pick.astype(BF)) * pick, axis=1, keepdims=True).astype(I32) - 1
    slot_col_ref[...] = jnp.where(live, eid[:, :1] * capacity + rank, experts * capacity)

    own_g.wait()
    for copy in (normed_copy, qkv_copy, mixed_copy, laug_copy, h_copy, slots_copy):
        copy.wait()

    @pl.loop(1, experts)
    def _(j):
        g_copy(j).wait()


def place(slot_row_ref, src_ref, slots_ref, c, step):
    seq = src_ref.shape[0]
    index = lax.broadcasted_iota(I32, (step, seq), 0) + c * step
    onehot = jnp.where(index == slot_row_ref[...], 1.0, 0.0).astype(BF)
    slots_ref[rows_of(c, step), :] = dot(onehot, src_ref[...]).astype(BF)


def collect(slot_col_ref, ret_ref, r):
    total = ret_ref.shape[0]
    onehot = jnp.where(slot_col_ref[r, :] == lane_iota((ROWS, total)), 1.0, 0.0).astype(BF)
    return dot(onehot, ret_ref[...])


def flip(v, j, size):
    out, bit = 0, 1
    while bit < size:
        out = out + bit * ((v // bit + j // bit) % 2)
        bit *= 2
    return out


def greet(experts, with_partner):
    me = lax.axis_index("expert")
    barrier = pltpu.get_barrier_semaphore()

    @pl.loop(1, experts)
    def _(j):
        pl.semaphore_signal(
            barrier, inc=1, device_id={"expert": flip(me, j, experts)}, device_id_type=MESH
        )

    if with_partner:
        pl.semaphore_signal(
            barrier, inc=1, device_id={"dp": 1 - lax.axis_index("dp")}, device_id_type=MESH
        )
    pl.semaphore_wait(barrier, experts - 1 + int(with_partner))


def expert_kernel(
    experts, capacity,
    x_ref, g_ref, win_hbm, wback_hbm,
    ing_ref, ffn_ref, ffn_got, wing_ref, wbg_ref,
    xin, gin, win, wback, hidden, act, ing_out, xt, own_in, own_back, got_in, got_back,
    x_send, x_recv, r_send, r_recv, f_send, f_recv, g_sem, w_sem, own_sem, ffn_sem, t_send, t_recv, o_sem,
):
    me = lax.axis_index("expert")
    other = 1 - lax.axis_index("dp")
    width, ff = win.shape
    groups, chunk = experts // 4, 4 * capacity

    def block(j):
        return pl.ds(pl.multiple_of(j * capacity, 16), capacity)

    def x_copy(j):
        peer = flip(me, j, experts)
        return pltpu.make_async_remote_copy(
            src_ref=x_ref.at[block(peer)], dst_ref=xin.at[block(j)],
            send_sem=x_send.at[j], recv_sem=x_recv.at[j],
            device_id={"expert": peer}, device_id_type=MESH,
        )

    def r_copy(j):
        return pltpu.make_async_remote_copy(
            src_ref=ing_out.at[block(j)], dst_ref=ing_ref.at[block(me)],
            send_sem=r_send.at[j], recv_sem=r_recv.at[j],
            device_id={"expert": flip(me, j, experts)}, device_id_type=MESH,
        )

    load_g = pltpu.make_async_copy(g_ref, gin, g_sem)

    own_x = pltpu.make_async_copy(x_ref.at[block(me)], xin.at[block(0)], own_sem.at[0])
    own_ing = pltpu.make_async_copy(ing_out.at[block(0)], ing_ref.at[block(me)], own_sem.at[1])
    load_in = pltpu.make_async_copy(win_hbm, win, w_sem.at[0])
    load_back = pltpu.make_async_copy(wback_hbm, wback, w_sem.at[1])
    own_x.start()
    load_in.start()
    load_back.start()

    load_g.start()

    greet(experts, True)
    for low, high in ((2, 3), (0, 2), (3, 4)):

        @pl.loop(max(1, experts * low // 4), experts * high // 4)
        def _(j):
            x_copy(j).start()

    own_x.wait()
    load_in.wait()
    load_back.wait()

    load_g.wait()

    def ffn_copy(j):
        peer = flip(me, j, experts)
        return pltpu.make_async_copy(xin.at[block(j)], ffn_ref.at[block(peer)], ffn_sem.at[j])

    def ffn_near(j):
        return pltpu.make_async_remote_copy(
            src_ref=xin.at[block(j)], dst_ref=ffn_got.at[block(me)],
            send_sem=f_send.at[j], recv_sem=f_recv.at[j],
            device_id={"expert": flip(me, j, experts)}, device_id_type=MESH,
        )

    own_ffn = pltpu.make_async_copy(xin.at[block(0)], ffn_got.at[block(me)], own_sem.at[0])

    @pl.loop(0, groups)
    def _(i):
        r = rows_of(i, chunk)
        for c in range(4):
            j = 4 * i + c

            @pl.when(j > 0)
            def _():
                x_copy(j).wait_recv()

        @pl.loop(0, ff // 512)
        def _(t):
            c = rows_of(t, 512)
            a = dot(xin[r, :], win[:, c])
            gate = jax.nn.sigmoid(a)
            hidden[r, c] = (a * gate).astype(BF)
            back = dot_t(gin[r, :], wback[c, :])
            act[r, c] = (back * gate * (1.0 + a * (1.0 - gate))).astype(BF)

        @pl.loop(0, width // 256)
        def _(n):
            c = rows_of(n, 256)
            ing_out[r, c] = dot_t(act[r, :], win[c, :]).astype(BF)

        for c in range(4):
            j = 4 * i + c

            @pl.when(j > 0)
            def _():
                r_copy(j).start()

        @pl.when(i == 0)
        def _():
            own_ing.start()

        xt[:, r] = xin[r, :].T

        @pl.loop(0, width // 256)
        def _(n):
            c = rows_of(n, 256)
            xin[r, c] = dot(hidden[r, :], wback[:, c]).astype(BF)

        for c in range(4):
            j = 4 * i + c

            @pl.when(j >= experts // 2)
            def _():
                ffn_copy(j).start()

            @pl.when((j > 0) & (j < experts // 2))
            def _():
                ffn_near(j).start()

        @pl.when(i == 0)
        def _():
            own_ffn.start()

    tiles = ff // 256

    def sends(t):
        s = t % 4
        to = dict(device_id={"dp": other}, device_id_type=MESH)
        return (
            pltpu.make_async_remote_copy(own_in.at[s], got_in.at[t], t_send.at[0, t], t_recv.at[0, t], **to),
            pltpu.make_async_remote_copy(own_back.at[s], got_back.at[t], t_send.at[1, t], t_recv.at[1, t], **to),
        )

    def writes(t):
        s, c = t % 4, rows_of(t, 256)
        return (
            pltpu.make_async_copy(own_in.at[s], wing_ref.at[:, c], o_sem.at[0, s]),
            pltpu.make_async_copy(own_back.at[s], wbg_ref.at[c, :], o_sem.at[1, s]),
        )

    @pl.loop(0, tiles + 2)
    def _(t):
        @pl.when(t < tiles)
        def _():
            s, c = t % 4, rows_of(t, 256)

            @pl.when(t >= 4)
            def _():
                for copy in writes(t - 4):
                    copy.wait()

            own_in[s] = dot(xt[...], act[:, c]).astype(BF)
            own_back[s] = tdot(hidden[:, c], gin[...]).astype(BF)
            for copy in sends(t):
                copy.start()

        @pl.when(t >= 2)
        def _():
            u = t - 2
            for copy in sends(u):
                copy.wait()
            s = u % 4
            own_in[s] = (own_in[s].astype(F32) + got_in[u].astype(F32)).astype(BF)
            own_back[s] = (own_back[s].astype(F32) + got_back[u].astype(F32)).astype(BF)
            for copy in writes(u):
                copy.start()

    for u in range(tiles - 4, tiles):
        for copy in writes(u):
            copy.wait()
    own_ing.wait()

    own_ffn.wait()

    @pl.loop(experts // 2, experts)
    def _(j):
        ffn_copy(j).wait()

    @pl.loop(1, experts // 2)
    def _(j):
        ffn_near(j).wait()

    @pl.loop(1, experts)
    def _(j):
        x_copy(j).wait_send()
        r_copy(j).wait()


def forward_call(experts, capacity, lengths, eid_row, g1, g2, x, g, w_qkv, w_out):
    seq, width = x.shape
    pairs, total = width // LANES, experts * capacity
    dma = pltpu.SemaphoreType.DMA
    vmem = pltpu.VMEM
    return pl.pallas_call(
        functools.partial(forward_kernel, experts, capacity),
        out_shape=(
            sds((seq, width), BF),
            sds((3 * pairs, seq, LANES), BF),
            sds((seq, width), BF),
            sds((pairs, seq, LANES), BF),
            sds((seq, width), F32),
            sds((total, width), BF),
            sds((seq, 1), I32),
            sds((total, width), BF),
        ),
        in_specs=[SMEM] + [VMEM] * 3 + [ANY] * 4,
        out_specs=(ANY,) * 6 + (VMEM, ANY),
        scratch_shapes=[
            vmem((seq, width), BF),
            vmem((seq, width), BF),
            vmem((width, 3 * width), BF),
            vmem((width, width), BF),
            vmem((seq, width), BF),
            vmem((3 * pairs, seq, LANES), BF),
            vmem((seq, width), BF),
            vmem((pairs, seq, LANES), BF),
            vmem((seq, width), F32),
            vmem((total, width), BF),
            vmem((seq, LANES), BF),
            vmem((seq, width), BF),
            vmem((1, seq), I32),
            vmem((total, width), BF),
            dma((4,)), dma((6,)), dma, dma((experts,)), dma((experts,)),
        ],
        compiler_params=params(60, collective_id=4, has_side_effects=True),
        cost_estimate=pl.CostEstimate(flops=40 * 10**9, bytes_accessed=24 * 10**6, transcendentals=0),
        name="attention_forward",
    )(lengths, eid_row, g1, g2, x, g, w_qkv, w_out)


def experts_call(experts, capacity, x_slots, g_slots, w_in, w_back):
    total, width = x_slots.shape
    ff = w_in.shape[1]
    tiles = ff // 256
    dma = pltpu.SemaphoreType.DMA
    return pl.pallas_call(
        functools.partial(expert_kernel, experts, capacity),
        out_shape=(
            sds((total, width), BF), sds((total, width), BF), sds((total, width), BF),
            sds((width, ff), BF), sds((ff, width), BF),
        ),
        in_specs=[ANY] * 4,
        out_specs=(ANY,) * 5,
        scratch_shapes=[
            pltpu.VMEM((total, width), BF),
            pltpu.VMEM((total, width), BF),
            pltpu.VMEM((width, ff), BF),
            pltpu.VMEM((ff, width), BF),
            pltpu.VMEM((total, ff), BF),
            pltpu.VMEM((total, ff), BF),
            pltpu.VMEM((total, width), BF),
            pltpu.VMEM((width, total), BF),
            pltpu.VMEM((4, width, 256), BF),
            pltpu.VMEM((4, 256, width), BF),
            pltpu.VMEM((tiles, width, 256), BF),
            pltpu.VMEM((tiles, 256, width), BF),
            dma((experts,)), dma((experts,)), dma((experts,)), dma((experts,)),
            dma((experts // 2,)), dma((experts // 2,)),
            dma, dma((2,)), dma((2,)), dma((experts,)),
            dma((2, tiles)), dma((2, tiles)), dma((2, 4)),
        ],
        compiler_params=params(61, collective_id=1, has_side_effects=True),
        cost_estimate=pl.CostEstimate(flops=44 * 10**9, bytes_accessed=30 * 10**6, transcendentals=0),
        name="experts",
    )(x_slots, g_slots, w_in, w_back)


def unit_plan(width):
    pairs = width // LANES
    third = pairs // 3
    runs = [tuple(3 * pairs + third * n + m for m in range(third)) for n in range(3)]
    runs += [(n * pairs + p,) for p in range(pairs) for n in range(3)]
    plan, row = [], 0
    for run in runs:
        count = len(run) * width + (0 if plan else 16 * pairs)
        piece = -(-count // (2 * INNER * 16)) * 16
        plan.append((row, run, piece))
        row += 2 * INNER * piece
    return plan, row


def backward_kernel(
    experts, capacity,
    len_ref, g1_ref, g2_ref, tok_hbm, cot_hbm, normed_hbm, qkv_hbm, mixed_hbm, laug_hbm, h_hbm, ret_hbm, slot_col_ref,
    wqkv_hbm, wout_hbm, ffn_hbm, got_hbm,
    out_ref, tokg_ref, sums_ref, g2g_ref,
    tok_ref, qkv_ref, mixed_ref, laug_ref, h_ref, ret_ref, wqkv_ref, wout_ref, ffn_ref,
    hgrad_ref, hg_ref, mg_ref, daug_ref, kaug_ref, dq_ref, qg_ref, normt_ref,
    part, final, got_core, got_pair, got_quad, got_out, g2_acc,
    load_sem, f_send, f_recv, core_send, core_recv, pair_send, pair_recv, quad_send, quad_recv, out_send, out_recv, o_sem,
):
    seq, width = tok_ref.shape
    blocks, pairs, total = seq // ROWS, width // LANES, experts * capacity
    me, core = lax.axis_index("expert"), lax.axis_index("dp")
    outer = experts // INNER
    far = me // INNER

    def spot(u):
        bit = u % 3
        low, high = [b for b in range(3) if b != bit]
        return bit, me // 2**bit % 2, me // 2**low % 2 + 2 * (me // 2**high % 2)


    plan, _ = unit_plan(width)
    first = lane_iota((1, LANES)) < HEAD

    def block(j):
        return pl.ds(pl.multiple_of(j * capacity, 16), capacity)

    def rows(start, size):
        return pl.ds(pl.multiple_of(start, 16), size)

    def ffn_copy(j):
        peer = flip(me, j, experts)
        return pltpu.make_async_remote_copy(
            src_ref=ffn_hbm.at[block(peer)], dst_ref=ffn_ref.at[block(me)],
            send_sem=f_send.at[j], recv_sem=f_recv.at[j],
            device_id={"expert": peer}, device_id_type=MESH,
        )

    close = pl.ds(pl.multiple_of(me // (experts // 2) * total // 2, 16), total // 2)
    near_ffn = pltpu.make_async_copy(got_hbm.at[close], ffn_ref.at[close], load_sem.at[0])
    loads = [
        pltpu.make_async_copy(src, dst, load_sem.at[1 + i])
        for i, (src, dst) in enumerate(
            (
                (ret_hbm, ret_ref),
                (h_hbm, h_ref),
                (cot_hbm, tok_ref),
                (wout_hbm, wout_ref),
                (mixed_hbm, mixed_ref),
                (normed_hbm, qg_ref.at[:, :width]),
                (qkv_hbm, qkv_ref),
                (laug_hbm, laug_ref),
                (wqkv_hbm, wqkv_ref),
            )
        )
    ]
    for copy in loads[:5]:
        copy.start()
    load_tok = pltpu.make_async_copy(tok_hbm, tok_ref, load_sem.at[10])
    greet(experts, True)

    def send_ffn(r):
        share = experts // 16
        for j in range(r * share, (r + 1) * share):
            ffn_copy(experts // 2 + j).start()

    send_ffn(0)
    send_ffn(1)
    near_ffn.start()
    for copy in loads[5:]:
        copy.start()

    def core_copy(u, back):
        start, _, piece = plan[u]
        half = INNER * piece
        src = final if back else part
        mine, theirs = start + core * half, start + (1 - core) * half
        return pltpu.make_async_remote_copy(
            src_ref=src.at[rows(mine if back else theirs, half)],
            dst_ref=final.at[rows(mine, half)] if back else got_core.at[rows(start // 2, half)],
            send_sem=core_send.at[u, back], recv_sem=core_recv.at[u, back],
            device_id={"dp": 1 - core}, device_id_type=MESH,
        )

    def pair_copy(u, back):
        start, _, piece = plan[u]
        bit, side, _ = spot(u)
        base = start + core * INNER * piece
        own = final.at[rows(base + side * 4 * piece, 4 * piece)]
        return pltpu.make_async_remote_copy(
            src_ref=own if back else part.at[rows(base + (1 - side) * 4 * piece, 4 * piece)],
            dst_ref=own if back else got_pair.at[rows(start // 4, 4 * piece)],
            send_sem=pair_send.at[u, back], recv_sem=pair_recv.at[u, back],
            device_id={"expert": flip(me, 2**bit, experts)}, device_id_type=MESH,
        )

    def quad_copy(u, back, i):
        start, _, piece = plan[u]
        bit, side, place = spot(u)
        low, high = [b for b in range(3) if b != bit]
        base = start + (core * INNER + side * 4) * piece
        own = final.at[rows(base + place * piece, piece)]
        return pltpu.make_async_remote_copy(
            src_ref=own if back else part.at[rows(base + flip(place, i, 4) * piece, piece)],
            dst_ref=own if back else got_quad.at[i - 1, rows(start // (2 * INNER), piece)],
            send_sem=quad_send.at[u, back, i], recv_sem=quad_recv.at[u, back, i],
            device_id={"expert": flip(me, i % 2 * 2**low + i // 2 * 2**high, experts)}, device_id_type=MESH,
        )

    def outer_copy(u, i):
        start, _, piece = plan[u]
        own = got_out.at[far, rows(start // (2 * INNER), piece)]
        return pltpu.make_async_remote_copy(
            src_ref=own, dst_ref=own,
            send_sem=out_send.at[u, i], recv_sem=out_recv.at[u, i],
            device_id={"expert": flip(me, i * INNER, experts)}, device_id_type=MESH,
        )

    def add_up(to, sources, size):
        step = 16 * max(k for k in range(1, 13) if size // 16 % k == 0)

        @pl.loop(0, size // step)
        def _(n):
            r = rows_of(n, step)
            total = sources[0][r, :].astype(F32)
            for source in sources[1:]:
                total = total + source[r, :].astype(F32)
            to[r, :] = total.astype(BF)

    def advance(u, stage):
        start, _, piece = plan[u]
        half = INNER * piece
        _, side, place = spot(u)
        mine = part.at[rows(start + core * half, half)]
        quarter = part.at[rows(start + core * half + side * 4 * piece, 4 * piece)]
        at = rows(start + core * half + (side * 4 + place) * piece, piece)
        shared = rows(start // (2 * INNER), piece)
        if stage == 0:
            core_copy(u, 0).start()
        elif stage == 1:
            core_copy(u, 0).wait()
            add_up(mine, [mine, got_core.at[rows(start // 2, half)]], half)
            pair_copy(u, 0).start()
        elif stage == 2:
            pair_copy(u, 0).wait()
            add_up(quarter, [quarter, got_pair.at[rows(start // 4, 4 * piece)]], 4 * piece)
            for i in range(1, 4):
                quad_copy(u, 0, i).start()
        elif stage == 3:
            for i in range(1, 4):
                quad_copy(u, 0, i).wait()
            add_up(got_out.at[far, shared], [part.at[at]] + [got_quad.at[i, shared] for i in range(3)], piece)
            for i in range(1, outer):
                outer_copy(u, i).start()
        elif stage == 4:
            for i in range(1, outer):
                outer_copy(u, i).wait()
            add_up(final.at[at], [got_out.at[o, shared] for o in range(outer)], piece)
            for i in range(1, 4):
                quad_copy(u, 1, i).start()
        elif stage == 5:
            for i in range(1, 4):
                quad_copy(u, 1, i).wait()
            pair_copy(u, 1).start()
        elif stage == 6:
            pair_copy(u, 1).wait()
            core_copy(u, 1).start()
        else:
            core_copy(u, 1).wait()
            for copy in sums_copies(u):
                copy.start()

    def sums_copies(u):
        start, tiles, _ = plan[u]
        return [
            pltpu.make_async_copy(final.at[start + i * width : start + (i + 1) * width], sums_ref.at[tile], o_sem.at[tile])
            for i, tile in enumerate(tiles)
        ]

    for copy in loads[:5]:
        copy.wait()

    g2_acc[...] = jnp.zeros_like(g2_acc)

    @pl.loop(0, blocks)
    def _(i):
        r = rows_of(i)
        hat, inverse = normalize(h_ref[r, :])
        ing = collect(slot_col_ref, ret_ref, r)
        g2_acc[...] += jnp.sum((ing * hat).reshape(ROWS // 8, 8, width), axis=0)
        grad = tok_ref[r, :].astype(F32) + norm_back(ing * g2_ref[...].reshape(1, width), hat, inverse)
        hgrad_ref[r, :] = grad
        low = grad.astype(BF)
        hg_ref[r, :] = low
        mg = dot_t(low, wout_ref[...]).astype(BF)

        @pl.when(i == blocks // 2)
        def _():
            send_ffn(2)

        for p in range(pairs):
            piece = mg[:, p * LANES : (p + 1) * LANES]
            mg_ref[p, r, :] = piece
            prod = piece.astype(F32) * mixed_ref[r, p * LANES : (p + 1) * LANES].astype(F32)
            zero = jnp.zeros_like(prod)
            d0 = jnp.sum(jnp.where(first, prod, zero), axis=1, keepdims=True)
            d1 = jnp.sum(jnp.where(first, zero, prod), axis=1, keepdims=True)
            daug_ref[p, r, :] = aug_of(jnp.where(first, d1, d0), 0.0)

    load_tok.start()

    gain_at = len(plan[0][1]) * width
    spare = 2 * INNER * plan[0][2] - gain_at
    part[gain_at : gain_at + spare, :] = jnp.zeros((spare, LANES), BF)
    for p in range(pairs):
        gain = jnp.sum(g2_acc[:, p * LANES : (p + 1) * LANES], axis=0, keepdims=True)
        part[gain_at + 16 * p : gain_at + 16 * p + 1, :] = gain.astype(BF)

    @pl.loop(0, width // 256)
    def _(n):
        out = tdot(mixed_ref[...], hg_ref[:, rows_of(n, 256)]).astype(BF)
        for m in range(2):
            tile = 2 * n + m
            third = pairs // 3
            at = tile * width + jnp.where(tile < third, 0, spare)
            part[rows(at, width), :] = out[:, m * LANES : (m + 1) * LANES]

    send_ffn(3)
    for n in range(3):
        advance(n, 0)
    loads[5].wait()

    @pl.loop(0, blocks)
    def _(i):
        r = rows_of(i)
        normt_ref[:, r] = qg_ref[r, :width].T

    kaug_ref[...] = key_aug(seq, len_ref[0])
    scale = jnp.asarray(HEAD**-0.5, BF)
    for copy in loads[6:]:
        copy.wait()

    ends = {}
    for unit, points in enumerate(STAGES):
        for stage, at in enumerate(points):
            ends.setdefault(at, []).extend((3 * unit + n, stage) for n in range(3))

    @pl.loop(0, pairs)
    def _(p):
        keep = lane_iota((ROWS, ROWS)) >= lax.broadcasted_iota(I32, (ROWS, ROWS), 0)
        vaug = jnp.where(lane_iota((ROWS, LANES)) % HEAD < 3, 1.0, 0.0).astype(BF)
        none = jnp.zeros((ROWS, LANES), BF)
        dq_ref[...] = jnp.zeros_like(dq_ref)
        for j in range(blocks):
            kr = slice(j * ROWS, (j + 1) * ROWS)
            qr = slice(j * ROWS, seq)
            q = qkv_ref[p, qr, :] * scale
            k = qkv_ref[pairs + p, kr, :]
            v = qkv_ref[2 * pairs + p, kr, :]
            do = mg_ref[p, qr, :]
            la, da = laug_ref[p, qr, :], daug_ref[p, qr, :]
            ka = kaug_ref[kr, :]
            dvs, dks, dss, kms = [], [], [], []
            for head in range(2):
                mine = first if head == 0 else ~first
                s = dot_t(jnp.where(mine, k, ka), jnp.where(mine, q, la))
                e = jnp.exp(s)
                start = jnp.where(keep, e[:, :ROWS], 0.0)
                e = jnp.concatenate([start, e[:, ROWS:]], axis=1) if j < blocks - 1 else start
                dp = dot_t(jnp.where(mine, v, vaug), jnp.where(mine, do, da))
                ds = (e * dp).astype(BF)
                dvs.append(dot(e.astype(BF), do))
                dks.append(dot(ds, q))
                dss.append(ds)
                kms.append(jnp.where(mine, k, none))
            qg_ref[kr, rows_of(2 * pairs + p, LANES)] = jnp.where(first, dvs[0], dvs[1]).astype(BF)
            qg_ref[kr, rows_of(pairs + p, LANES)] = jnp.where(first, dks[0], dks[1]).astype(BF)
            dq_ref[qr, :] += tdot(jnp.concatenate(dss, axis=0), jnp.concatenate(kms, axis=0))
        qg_ref[:, rows_of(p, LANES)] = (dq_ref[...] * HEAD**-0.5).astype(BF)

        tiles3 = [qg_ref[:, rows_of(n * pairs + p, LANES)] for n in range(3)]
        out = dot(normt_ref[...], jnp.concatenate(tiles3, axis=1)).astype(BF)
        for n in range(3):
            at = plan[3][0] + (3 * p + n) * width
            part[rows(at, width), :] = out[:, n * LANES : (n + 1) * LANES]

        for at in range(pairs):

            @pl.when(p == at)
            def _():
                if at < 4:
                    send_ffn(4 + at)
                for u, stage in ends.get(at, ()):
                    advance(u, stage)

    load_tok.wait()

    def finish_tokens(i):
        r = rows_of(i)
        n1 = dot_t(qg_ref[r, :], wqkv_ref[...])
        hat, inverse = normalize(tok_ref[r, :].astype(F32))
        hgrad_ref[r, :] = hgrad_ref[r, :] + norm_back(n1 * g1_ref[...].reshape(1, width), hat, inverse)
        tokg_copy(i).start()

    def tokg_copy(i):
        return pltpu.make_async_copy(hgrad_ref.at[rows_of(i)], tokg_ref.at[rows_of(i)], load_sem.at[1 + i])

    def finish_output(i):
        r = rows_of(i)
        h_ref[r, :] = h_ref[r, :] + collect(slot_col_ref, ffn_ref, r)
        out_copy(i).start()

    def out_copy(i):
        return pltpu.make_async_copy(h_ref.at[rows_of(i)], out_ref.at[rows_of(i)], load_sem.at[1 + blocks + i])

    for step in range(pairs, max(ends) + 1):
        for u, stage in ends[step]:
            advance(u, stage)
        n = step - pairs
        if n < blocks:
            finish_tokens(n)
        elif n < blocks + 2:
            if n == blocks:
                near_ffn.wait()

                @pl.loop(experts // 2, experts)
                def _(j):
                    ffn_copy(j).wait()

            for i in range((n - blocks) * blocks // 2, (n - blocks + 1) * blocks // 2):
                finish_output(i)

    for p in range(pairs):
        g2g_ref[p * LANES : (p + 1) * LANES] = final[gain_at + 16 * p : gain_at + 16 * p + 1, :].astype(F32).reshape(LANES)
    for i in range(blocks):
        tokg_copy(i).wait()
        out_copy(i).wait()
    for u in range(len(plan)):
        for copy in sums_copies(u):
            copy.wait()


def backward_call(experts, capacity, lengths, g1, g2, x, g, normed, qkv, mixed, laug, h, ret, slot_col, w_qkv, w_out, ffn, got):
    seq, width = x.shape
    pairs, total = width // LANES, experts * capacity
    plan, height = unit_plan(width)
    outer, units = experts // INNER, len(plan)
    dma = pltpu.SemaphoreType.DMA
    vmem = pltpu.VMEM
    return pl.pallas_call(
        functools.partial(backward_kernel, experts, capacity),
        out_shape=(
            sds((seq, width), F32), sds((seq, width), F32), sds((4 * pairs, width, LANES), BF), sds((width,), F32),
        ),
        in_specs=[SMEM, VMEM, VMEM] + [ANY] * 8 + [VMEM] + [ANY] * 4,
        out_specs=(ANY, ANY, ANY, VMEM),
        scratch_shapes=[
            vmem((seq, width), BF),
            vmem((3 * pairs, seq, LANES), BF),
            vmem((seq, width), BF),
            vmem((pairs, seq, LANES), BF),
            vmem((seq, width), F32),
            vmem((total, width), BF),
            vmem((width, 3 * width), BF),
            vmem((width, width), BF),
            vmem((total, width), BF),
            vmem((seq, width), F32),
            vmem((seq, width), BF),
            vmem((pairs, seq, LANES), BF),
            vmem((pairs, seq, LANES), BF),
            vmem((seq, LANES), BF),
            vmem((seq, LANES), F32),
            vmem((seq, 3 * width), BF),
            vmem((width, seq), BF),
            vmem((height, LANES), BF),
            vmem((height, LANES), BF),
            vmem((height // 2, LANES), BF),
            vmem((height // 4, LANES), BF),
            vmem((3, height // (2 * INNER), LANES), BF),
            vmem((outer, height // (2 * INNER), LANES), BF),
            vmem((8, width), F32),
            dma((11,)), dma((experts,)), dma((experts,)),
            dma((units, 2)), dma((units, 2)),
            dma((units, 2)), dma((units, 2)),
            dma((units, 2, 4)), dma((units, 2, 4)),
            dma((units, outer)), dma((units, outer)),
            dma((4 * pairs,)),
        ],
        compiler_params=params(62, collective_id=2, has_side_effects=True),
        cost_estimate=pl.CostEstimate(flops=60 * 10**9, bytes_accessed=24 * 10**6, transcendentals=0),
        name="attention_backward",
    )(lengths, g1, g2, x, g, normed, qkv, mixed, laug, h, ret, slot_col, w_qkv, w_out, ffn, got)


def finish_kernel(
    win_ref, wback_ref, sums_ref, wqkv_ref, g1_ref,
    win_out, wback_out, wqkv_out, wout_out, g1g_ref,
    gain_ref,
):
    i = pl.program_id(0)
    size = wqkv_ref.shape[0]
    tiles = sums_ref.shape[0]
    pairs = tiles // 4
    win_out[...] = win_ref[...].astype(F32)
    wback_out[...] = wback_ref[...].astype(F32)
    gain = jnp.zeros((size, LANES), F32)
    for t in range(tiles):
        tile = sums_ref[t].astype(F32)
        if t < 3 * pairs:
            c = slice(t * LANES, (t + 1) * LANES)
            wqkv_out[:, c] = tile
            gain = gain + tile * wqkv_ref[:, c].astype(F32)
        else:
            wout_out[:, (t - 3 * pairs) * LANES : (t - 3 * pairs + 1) * LANES] = tile
    gain_ref[rows_of(i, size), :] = gain

    @pl.when(i == pl.num_programs(0) - 1)
    def _():
        total = lax.dot_general(
            jnp.ones((8, LANES), F32), gain_ref[...], (((1,), (1,)), ((), ())),
            precision=lax.Precision.HIGHEST, preferred_element_type=F32,
        )
        g1g_ref[...] = (total[0] / g1_ref[...])


def finish_call(win, wback, sums, w_qkv, g1):
    width, ff = win.shape
    tiles, steps = sums.shape[0], 8
    wide = pl.BlockSpec((width // steps, ff), lambda i: (i, 0))
    tall = pl.BlockSpec((ff // steps, width), lambda i: (i, 0))
    three = pl.BlockSpec((width // steps, 3 * width), lambda i: (i, 0))
    square = pl.BlockSpec((width // steps, width), lambda i: (i, 0))
    row = pl.BlockSpec((width,), lambda i: (0,))
    return pl.pallas_call(
        finish_kernel,
        grid=(steps,),
        out_shape=(
            sds((width, ff), F32), sds((ff, width), F32), sds((width, 3 * width), F32), sds((width, width), F32),
            sds((width,), F32),
        ),
        in_specs=[wide, tall, pl.BlockSpec((tiles, width // steps, LANES), lambda i: (0, i, 0)), three, row],
        out_specs=(wide, tall, three, square, row),
        scratch_shapes=[pltpu.VMEM((width, LANES), F32)],
        compiler_params=params(61),
        name="finish_gradients",
    )(win, wback, sums, w_qkv, g1)


def params(mib, **kw):
    return pltpu.CompilerParams(vmem_limit_bytes=mib * MIB, **kw)


def sds(shape, dtype):
    return jax.ShapeDtypeStruct(shape, dtype)


def shards(experts, tokens, lengths, expert_ids, w_qkv, w_out, norm1_gain, norm2_gain, w_in, w_back, cotangent):
    x, g = tokens[0], cotangent[0]
    seq, width = x.shape
    pairs = width // LANES
    capacity = 3 * seq // (2 * experts)
    capacity = (capacity + 15) // 16 * 16
    total = experts * capacity
    eid_row = expert_ids.reshape(1, seq)
    g1, g2 = norm1_gain, norm2_gain

    normed, qkv, mixed, laug, h, x_slots, slot_col, g_in = forward_call(
        experts, capacity, lengths, eid_row, g1, g2, x, g, w_qkv, w_out
    )
    ing_ret, ffn, got, wing, wbg = experts_call(experts, capacity, x_slots, g_in, w_in[0], w_back[0])
    output, tokg, sums, g2_sum = backward_call(
        experts, capacity, lengths, g1, g2, x, g, normed, qkv, mixed, laug, h, ing_ret, slot_col, w_qkv, w_out, ffn, got
    )
    in_sum, back_sum, qkv_sum, out_sum, g1_sum = finish_call(wing, wbg, sums, w_qkv, g1)
    return (
        output[None], tokg[None], qkv_sum, out_sum, g1_sum, g2_sum, in_sum[None], back_sum[None],
    )


def solution(mesh):
    split = P(("dp", "expert"), None, None)
    mine = P("expert", None, None)
    return jax.shard_map(
        functools.partial(shards, mesh.shape["expert"]),
        mesh=mesh,
        in_specs=(split, P(("dp", "expert")), split, P(), P(), P(), P(), mine, mine, split),
        out_specs=(split, split, P(), P(), P(), P(), mine, mine),
        check_vma=False,
    )
```

```python
import functools

import jax
import jax.numpy as jnp
from jax import lax
from jax.experimental import pallas as pl
from jax.experimental.pallas import tpu as pltpu
from jax.sharding import PartitionSpec as P

BF, F32, I32 = jnp.bfloat16, jnp.float32, jnp.int32
HEAD = 64
LANES = 128
ROWS = 256
EPS = 1e-5
INNER = 8
STAGES = ((-1, 0, 1, 2, 4, 5, 6, 7), (1, 2, 3, 4, 5, 6, 7, 8), (3, 4, 5, 6, 7, 8, 9, 10), (4, 5, 6, 7, 8, 9, 10, 11), (5, 6, 7, 8, 9, 10, 11, 12))
NEG = -1e30
VMEM = pl.BlockSpec(memory_space=pltpu.VMEM)
ANY = pl.BlockSpec(memory_space=pl.ANY)
MESH = pl.DeviceIdType.MESH
SMEM = pl.BlockSpec(memory_space=pltpu.SMEM)
MIB = 2**20


def dot(a, b):
    return lax.dot_general(a, b, (((1,), (0,)), ((), ())), preferred_element_type=F32)


def dot_t(a, b):
    return lax.dot_general(a, b, (((1,), (1,)), ((), ())), preferred_element_type=F32)


def tdot(a, b):
    return lax.dot_general(a, b, (((0,), (0,)), ((), ())), preferred_element_type=F32)


def rows_of(i, n=ROWS):
    return pl.ds(pl.multiple_of(i * n, n), n)


def normalize(x):
    center = x - jnp.mean(x, axis=-1, keepdims=True)
    inverse = lax.rsqrt(jnp.mean(center * center, axis=-1, keepdims=True) + EPS)
    return center * inverse, inverse


def norm_back(u, hat, inverse):
    return inverse * (
        u - jnp.mean(u, axis=-1, keepdims=True) - hat * jnp.mean(u * hat, axis=-1, keepdims=True)
    )


def lane_iota(shape):
    return lax.broadcasted_iota(I32, shape, len(shape) - 1)


def split_parts(x):
    high = x.astype(BF)
    rest = x - high.astype(F32)
    middle = rest.astype(BF)
    low = (rest - middle.astype(F32)).astype(BF)
    return high, middle, low


def aug_of(x, one):
    high, middle, low = split_parts(x)
    lane = lane_iota(x.shape) % HEAD
    parts = jnp.where(
        lane == 0,
        -high.astype(F32),
        jnp.where(
            lane == 1,
            -middle.astype(F32),
            jnp.where(lane == 2, -low.astype(F32), jnp.where(lane == 3, one, 0.0)),
        ),
    )
    return parts.astype(BF)


def key_aug(seq, length):
    lane = lane_iota((seq, LANES)) % HEAD
    row = lax.broadcasted_iota(I32, (seq, LANES), 0)
    dead = jnp.where(row < length, 0.0, NEG)
    return jnp.where(lane < 3, 1.0, jnp.where(lane == 3, dead, 0.0)).astype(BF)


def forward_kernel(
    experts, capacity,
    len_ref, eid_row_ref, g1_ref, g2_ref, tok_hbm, cot_hbm, wqkv_hbm, wout_hbm,
    normed_out, qkv_out, mixed_out, laug_out, h_out, slots_out, slot_col_ref, g_got,
    tok_ref, cot_ref, wqkv_ref, wout_ref, normed_ref, qkv_ref, mixed_ref, laug_ref, h_ref, slots_ref,
    kaug_ref, xin_ref, slot_row_ref, gs_ref,
    load_sem, store_sem, own_sem, g_send, g_recv,
):
    seq, width = tok_ref.shape
    blocks, pairs = seq // ROWS, width // LANES
    total = experts * capacity
    groups, chunk = experts // 4, 4 * capacity
    length = len_ref[0]
    me = lax.axis_index("expert")

    def block(j):
        return pl.ds(pl.multiple_of(j * capacity, 16), capacity)

    def g_copy(j):
        peer = flip(me, j, experts)
        return pltpu.make_async_remote_copy(
            src_ref=gs_ref.at[block(peer)], dst_ref=g_got.at[block(j)],
            send_sem=g_send.at[j], recv_sem=g_recv.at[j],
            device_id={"expert": peer}, device_id_type=MESH,
        )

    own_g = pltpu.make_async_copy(gs_ref.at[block(me)], g_got.at[block(0)], own_sem)
    loads = [
        pltpu.make_async_copy(src, dst, load_sem.at[i])
        for i, (src, dst) in enumerate(
            ((cot_hbm, cot_ref), (tok_hbm, tok_ref), (wqkv_hbm, wqkv_ref), (wout_hbm, wout_ref))
        )
    ]
    for copy in loads:
        copy.start()
    normed_copy, qkv_copy, mixed_copy, laug_copy, h_copy, slots_copy = [
        pltpu.make_async_copy(src, dst, store_sem.at[i])
        for i, (src, dst) in enumerate(
            (
                (normed_ref, normed_out), (qkv_ref, qkv_out), (mixed_ref, mixed_out), (laug_ref, laug_out),
                (h_ref, h_out), (slots_ref, slots_out),
            )
        )
    ]

    tri = jnp.where(
        lax.broadcasted_iota(I32, (seq, seq), 0) <= lane_iota((seq, seq)), 1.0, 0.0
    ).astype(BF)
    eid = eid_row_ref[...]
    live = lane_iota((1, seq)) < length
    pick = (lax.broadcasted_iota(I32, (experts, seq), 0) == eid) & live
    pick = jnp.where(pick, 1.0, 0.0)
    rank = jnp.sum(dot(pick.astype(BF), tri) * pick, axis=0, keepdims=True).astype(I32) - 1
    slot_row_ref[...] = jnp.where(live, eid * capacity + rank, total)

    greet(experts, False)
    loads[0].wait()

    def send_group(n):
        place(slot_row_ref, cot_ref, gs_ref, flip(me // 4, n, groups), chunk)
        for c in range(4):
            j = 4 * n + c

            @pl.when(j > 0)
            def _():
                g_copy(j).start()

        @pl.when(n == 0)
        def _():
            own_g.start()

    for low, high in ((groups // 2, groups), (0, groups // 2)):

        @pl.loop(low, high)
        def _(n):
            send_group(n)

    for copy in loads[1:]:
        copy.wait()

    @pl.loop(0, blocks)
    def _(i):
        hat, _ = normalize(tok_ref[rows_of(i), :].astype(F32))
        normed_ref[rows_of(i), :] = (hat * g1_ref[...].reshape(1, width)).astype(BF)

    @pl.loop(0, 3 * pairs // 2)
    def _(j):
        w = wqkv_ref[:, rows_of(j, 2 * LANES)]
        for i in range(blocks):
            r = slice(i * ROWS, (i + 1) * ROWS)
            out = dot(normed_ref[r, :], w).astype(BF)
            qkv_ref[2 * j, r, :] = out[:, :LANES]
            qkv_ref[2 * j + 1, r, :] = out[:, LANES:]

    normed_copy.start()
    qkv_copy.start()
    kaug_ref[...] = key_aug(seq, length)
    first = lane_iota((1, LANES)) < HEAD
    scale = jnp.asarray(HEAD**-0.5, BF)

    @pl.loop(0, pairs)
    def _(p):
        qaug = jnp.where(lane_iota((ROWS, LANES)) % HEAD == 3, 1.0, 0.0).astype(BF)
        causal = lane_iota((ROWS, ROWS)) <= lax.broadcasted_iota(I32, (ROWS, ROWS), 0)
        one = jnp.ones((1, LANES), BF)
        for i in range(blocks):
            r = slice(i * ROWS, (i + 1) * ROWS)
            n = (i + 1) * ROWS
            q = qkv_ref[p, r, :] * scale
            k = qkv_ref[pairs + p, :n, :]
            v = qkv_ref[2 * pairs + p, :n, :]
            aug = kaug_ref[:n, :]
            outs, tops = [], []
            for head in range(2):
                mine = first if head == 0 else ~first
                s = dot_t(jnp.where(mine, q, qaug), jnp.where(mine, k, aug))
                last = jnp.where(causal, s[:, n - ROWS :], NEG)
                s = jnp.concatenate([s[:, : n - ROWS], last], axis=1) if i else last
                top = jnp.max(s, axis=1, keepdims=True)
                e = jnp.exp(s - top).astype(BF)
                outs.append(dot(e, jnp.where(mine, v, one)))
                tops.append(top)
            above = jnp.where(first, outs[0], outs[1])
            below = jnp.where(first, outs[1], outs[0])
            mixed_ref[r, rows_of(p, LANES)] = (above / pltpu.roll(below, HEAD, 1)).astype(BF)
            lse = jnp.where(first, tops[1], tops[0]) + jnp.log(below)
            laug_ref[p, r, :] = aug_of(lse, 1.0)

    mixed_copy.start()
    laug_copy.start()

    @pl.loop(0, blocks)
    def _(i):
        r = rows_of(i)
        h = tok_ref[r, :].astype(F32) + dot(mixed_ref[r, :], wout_ref[...])
        h_ref[r, :] = h
        hat, _ = normalize(h)
        xin_ref[r, :] = (hat * g2_ref[...].reshape(1, width)).astype(BF)

    h_copy.start()

    @pl.loop(0, groups)
    def _(n):
        place(slot_row_ref, xin_ref, slots_ref, n, chunk)

    slots_copy.start()
    eid = jnp.broadcast_to(eid_row_ref[...].astype(F32), (LANES, seq)).T.astype(I32)
    live = lax.broadcasted_iota(I32, (seq, 1), 0) < length
    pick = (lane_iota((seq, LANES)) == eid) & live
    pick = jnp.where(pick, 1.0, 0.0)
    rank = jnp.sum(tdot(tri, pick.astype(BF)) * pick, axis=1, keepdims=True).astype(I32) - 1
    slot_col_ref[...] = jnp.where(live, eid[:, :1] * capacity + rank, experts * capacity)

    own_g.wait()
    for copy in (normed_copy, qkv_copy, mixed_copy, laug_copy, h_copy, slots_copy):
        copy.wait()

    @pl.loop(1, experts)
    def _(j):
        g_copy(j).wait()


def place(slot_row_ref, src_ref, slots_ref, c, step):
    seq = src_ref.shape[0]
    index = lax.broadcasted_iota(I32, (step, seq), 0) + c * step
    onehot = jnp.where(index == slot_row_ref[...], 1.0, 0.0).astype(BF)
    slots_ref[rows_of(c, step), :] = dot(onehot, src_ref[...]).astype(BF)


def collect(slot_col_ref, ret_ref, r):
    total = ret_ref.shape[0]
    onehot = jnp.where(slot_col_ref[r, :] == lane_iota((ROWS, total)), 1.0, 0.0).astype(BF)
    return dot(onehot, ret_ref[...])


def flip(v, j, size):
    out, bit = 0, 1
    while bit < size:
        out = out + bit * ((v // bit + j // bit) % 2)
        bit *= 2
    return out


def greet(experts, with_partner):
    me = lax.axis_index("expert")
    barrier = pltpu.get_barrier_semaphore()

    @pl.loop(1, experts)
    def _(j):
        pl.semaphore_signal(
            barrier, inc=1, device_id={"expert": flip(me, j, experts)}, device_id_type=MESH
        )

    if with_partner:
        pl.semaphore_signal(
            barrier, inc=1, device_id={"dp": 1 - lax.axis_index("dp")}, device_id_type=MESH
        )
    pl.semaphore_wait(barrier, experts - 1 + int(with_partner))


def expert_kernel(
    experts, capacity,
    x_ref, g_ref, win_hbm, wback_hbm,
    ing_ref, ffn_ref, ffn_got, wing_ref, wbg_ref,
    xin, gin, win, wback, hidden, act, ing_out, xt, own_in, own_back, got_in, got_back,
    x_send, x_recv, r_send, r_recv, f_send, f_recv, g_sem, w_sem, own_sem, ffn_sem, t_send, t_recv, o_sem,
):
    me = lax.axis_index("expert")
    other = 1 - lax.axis_index("dp")
    width, ff = win.shape
    groups, chunk = experts // 4, 4 * capacity

    def block(j):
        return pl.ds(pl.multiple_of(j * capacity, 16), capacity)

    def x_copy(j):
        peer = flip(me, j, experts)
        return pltpu.make_async_remote_copy(
            src_ref=x_ref.at[block(peer)], dst_ref=xin.at[block(j)],
            send_sem=x_send.at[j], recv_sem=x_recv.at[j],
            device_id={"expert": peer}, device_id_type=MESH,
        )

    def r_copy(j):
        return pltpu.make_async_remote_copy(
            src_ref=ing_out.at[block(j)], dst_ref=ing_ref.at[block(me)],
            send_sem=r_send.at[j], recv_sem=r_recv.at[j],
            device_id={"expert": flip(me, j, experts)}, device_id_type=MESH,
        )

    load_g = pltpu.make_async_copy(g_ref, gin, g_sem)

    own_x = pltpu.make_async_copy(x_ref.at[block(me)], xin.at[block(0)], own_sem.at[0])
    own_ing = pltpu.make_async_copy(ing_out.at[block(0)], ing_ref.at[block(me)], own_sem.at[1])
    load_in = pltpu.make_async_copy(win_hbm, win, w_sem.at[0])
    load_back = pltpu.make_async_copy(wback_hbm, wback, w_sem.at[1])
    own_x.start()
    load_in.start()
    load_back.start()

    load_g.start()

    greet(experts, True)
    for low, high in ((2, 3), (0, 2), (3, 4)):

        @pl.loop(max(1, experts * low // 4), experts * high // 4)
        def _(j):
            x_copy(j).start()

    own_x.wait()
    load_in.wait()
    load_back.wait()

    load_g.wait()

    def ffn_copy(j):
        peer = flip(me, j, experts)
        return pltpu.make_async_copy(xin.at[block(j)], ffn_ref.at[block(peer)], ffn_sem.at[j])

    def ffn_near(j):
        return pltpu.make_async_remote_copy(
            src_ref=xin.at[block(j)], dst_ref=ffn_got.at[block(me)],
            send_sem=f_send.at[j], recv_sem=f_recv.at[j],
            device_id={"expert": flip(me, j, experts)}, device_id_type=MESH,
        )

    own_ffn = pltpu.make_async_copy(xin.at[block(0)], ffn_got.at[block(me)], own_sem.at[0])

    @pl.loop(0, groups)
    def _(i):
        r = rows_of(i, chunk)
        for c in range(4):
            j = 4 * i + c

            @pl.when(j > 0)
            def _():
                x_copy(j).wait_recv()

        @pl.loop(0, ff // 512)
        def _(t):
            c = rows_of(t, 512)
            a = dot(xin[r, :], win[:, c])
            gate = jax.nn.sigmoid(a)
            hidden[r, c] = (a * gate).astype(BF)
            back = dot_t(gin[r, :], wback[c, :])
            act[r, c] = (back * gate * (1.0 + a * (1.0 - gate))).astype(BF)

        @pl.loop(0, width // 256)
        def _(n):
            c = rows_of(n, 256)
            ing_out[r, c] = dot_t(act[r, :], win[c, :]).astype(BF)

        for c in range(4):
            j = 4 * i + c

            @pl.when(j > 0)
            def _():
                r_copy(j).start()

        @pl.when(i == 0)
        def _():
            own_ing.start()

        xt[:, r] = xin[r, :].T

        @pl.loop(0, width // 256)
        def _(n):
            c = rows_of(n, 256)
            xin[r, c] = dot(hidden[r, :], wback[:, c]).astype(BF)

        for c in range(4):
            j = 4 * i + c

            @pl.when(j >= experts // 2)
            def _():
                ffn_copy(j).start()

            @pl.when((j > 0) & (j < experts // 2))
            def _():
                ffn_near(j).start()

        @pl.when(i == 0)
        def _():
            own_ffn.start()

    tiles = ff // 256

    def sends(t):
        s = t % 4
        to = dict(device_id={"dp": other}, device_id_type=MESH)
        return (
            pltpu.make_async_remote_copy(own_in.at[s], got_in.at[t], t_send.at[0, t], t_recv.at[0, t], **to),
            pltpu.make_async_remote_copy(own_back.at[s], got_back.at[t], t_send.at[1, t], t_recv.at[1, t], **to),
        )

    def writes(t):
        s, c = t % 4, rows_of(t, 256)
        return (
            pltpu.make_async_copy(own_in.at[s], wing_ref.at[:, c], o_sem.at[0, s]),
            pltpu.make_async_copy(own_back.at[s], wbg_ref.at[c, :], o_sem.at[1, s]),
        )

    @pl.loop(0, tiles + 2)
    def _(t):
        @pl.when(t < tiles)
        def _():
            s, c = t % 4, rows_of(t, 256)

            @pl.when(t >= 4)
            def _():
                for copy in writes(t - 4):
                    copy.wait()

            own_in[s] = dot(xt[...], act[:, c]).astype(BF)
            own_back[s] = tdot(hidden[:, c], gin[...]).astype(BF)
            for copy in sends(t):
                copy.start()

        @pl.when(t >= 2)
        def _():
            u = t - 2
            for copy in sends(u):
                copy.wait()
            s = u % 4
            own_in[s] = (own_in[s].astype(F32) + got_in[u].astype(F32)).astype(BF)
            own_back[s] = (own_back[s].astype(F32) + got_back[u].astype(F32)).astype(BF)
            for copy in writes(u):
                copy.start()

    for u in range(tiles - 4, tiles):
        for copy in writes(u):
            copy.wait()
    own_ing.wait()

    own_ffn.wait()

    @pl.loop(experts // 2, experts)
    def _(j):
        ffn_copy(j).wait()

    @pl.loop(1, experts // 2)
    def _(j):
        ffn_near(j).wait()

    @pl.loop(1, experts)
    def _(j):
        x_copy(j).wait_send()
        r_copy(j).wait()


def forward_call(experts, capacity, lengths, eid_row, g1, g2, x, g, w_qkv, w_out):
    seq, width = x.shape
    pairs, total = width // LANES, experts * capacity
    dma = pltpu.SemaphoreType.DMA
    vmem = pltpu.VMEM
    return pl.pallas_call(
        functools.partial(forward_kernel, experts, capacity),
        out_shape=(
            sds((seq, width), BF),
            sds((3 * pairs, seq, LANES), BF),
            sds((seq, width), BF),
            sds((pairs, seq, LANES), BF),
            sds((seq, width), F32),
            sds((total, width), BF),
            sds((seq, 1), I32),
            sds((total, width), BF),
        ),
        in_specs=[SMEM] + [VMEM] * 3 + [ANY] * 4,
        out_specs=(ANY,) * 6 + (VMEM, ANY),
        scratch_shapes=[
            vmem((seq, width), BF),
            vmem((seq, width), BF),
            vmem((width, 3 * width), BF),
            vmem((width, width), BF),
            vmem((seq, width), BF),
            vmem((3 * pairs, seq, LANES), BF),
            vmem((seq, width), BF),
            vmem((pairs, seq, LANES), BF),
            vmem((seq, width), F32),
            vmem((total, width), BF),
            vmem((seq, LANES), BF),
            vmem((seq, width), BF),
            vmem((1, seq), I32),
            vmem((total, width), BF),
            dma((4,)), dma((6,)), dma, dma((experts,)), dma((experts,)),
        ],
        compiler_params=params(60, collective_id=4, has_side_effects=True),
        cost_estimate=pl.CostEstimate(flops=40 * 10**9, bytes_accessed=24 * 10**6, transcendentals=0),
        name="attention_forward",
    )(lengths, eid_row, g1, g2, x, g, w_qkv, w_out)


def experts_call(experts, capacity, x_slots, g_slots, w_in, w_back):
    total, width = x_slots.shape
    ff = w_in.shape[1]
    tiles = ff // 256
    dma = pltpu.SemaphoreType.DMA
    return pl.pallas_call(
        functools.partial(expert_kernel, experts, capacity),
        out_shape=(
            sds((total, width), BF), sds((total, width), BF), sds((total, width), BF),
            sds((width, ff), BF), sds((ff, width), BF),
        ),
        in_specs=[ANY] * 4,
        out_specs=(ANY,) * 5,
        scratch_shapes=[
            pltpu.VMEM((total, width), BF),
            pltpu.VMEM((total, width), BF),
            pltpu.VMEM((width, ff), BF),
            pltpu.VMEM((ff, width), BF),
            pltpu.VMEM((total, ff), BF),
            pltpu.VMEM((total, ff), BF),
            pltpu.VMEM((total, width), BF),
            pltpu.VMEM((width, total), BF),
            pltpu.VMEM((4, width, 256), BF),
            pltpu.VMEM((4, 256, width), BF),
            pltpu.VMEM((tiles, width, 256), BF),
            pltpu.VMEM((tiles, 256, width), BF),
            dma((experts,)), dma((experts,)), dma((experts,)), dma((experts,)),
            dma((experts // 2,)), dma((experts // 2,)),
            dma, dma((2,)), dma((2,)), dma((experts,)),
            dma((2, tiles)), dma((2, tiles)), dma((2, 4)),
        ],
        compiler_params=params(61, collective_id=1, has_side_effects=True),
        cost_estimate=pl.CostEstimate(flops=44 * 10**9, bytes_accessed=30 * 10**6, transcendentals=0),
        name="experts",
    )(x_slots, g_slots, w_in, w_back)


def unit_plan(width):
    pairs = width // LANES
    third = pairs // 3
    runs = [tuple(3 * pairs + third * n + m for m in range(third)) for n in range(3)]
    runs += [(n * pairs + p, n * pairs + p + 1) for p in range(0, pairs - 2, 2) for n in range(3)]
    runs += [(n * pairs + p,) for p in range(pairs - 2, pairs) for n in range(3)]
    plan, row = [], 0
    for run in runs:
        count = len(run) * width + (0 if plan else 16 * pairs)
        piece = -(-count // (2 * INNER * 16)) * 16
        plan.append((row, run, piece))
        row += 2 * INNER * piece
    return plan, row


def backward_kernel(
    experts, capacity,
    len_ref, g1_ref, g2_ref, tok_hbm, cot_hbm, normed_hbm, qkv_hbm, mixed_hbm, laug_hbm, h_hbm, ret_hbm, slot_col_ref,
    wqkv_hbm, wout_hbm, ffn_hbm, got_hbm,
    out_ref, tokg_ref, sums_ref, g2g_ref,
    tok_ref, qkv_ref, mixed_ref, laug_ref, h_ref, ret_ref, wqkv_ref, wout_ref, ffn_ref,
    hgrad_ref, hg_ref, mg_ref, daug_ref, kaug_ref, dq_ref, qg_ref, normt_ref,
    part, final, got_core, got_pair, got_quad, got_out, g2_acc,
    load_sem, f_send, f_recv, core_send, core_recv, pair_send, pair_recv, quad_send, quad_recv, out_send, out_recv, o_sem,
):
    seq, width = tok_ref.shape
    blocks, pairs, total = seq // ROWS, width // LANES, experts * capacity
    me, core = lax.axis_index("expert"), lax.axis_index("dp")
    outer = experts // INNER
    far = me // INNER

    def spot(u):
        bit = u % 3
        low, high = [b for b in range(3) if b != bit]
        return bit, me // 2**bit % 2, me // 2**low % 2 + 2 * (me // 2**high % 2)


    plan, _ = unit_plan(width)
    first = lane_iota((1, LANES)) < HEAD

    def block(j):
        return pl.ds(pl.multiple_of(j * capacity, 16), capacity)

    def rows(start, size):
        return pl.ds(pl.multiple_of(start, 16), size)

    def ffn_copy(j):
        peer = flip(me, j, experts)
        return pltpu.make_async_remote_copy(
            src_ref=ffn_hbm.at[block(peer)], dst_ref=ffn_ref.at[block(me)],
            send_sem=f_send.at[j], recv_sem=f_recv.at[j],
            device_id={"expert": peer}, device_id_type=MESH,
        )

    close = pl.ds(pl.multiple_of(me // (experts // 2) * total // 2, 16), total // 2)
    near_ffn = pltpu.make_async_copy(got_hbm.at[close], ffn_ref.at[close], load_sem.at[0])
    loads = [
        pltpu.make_async_copy(src, dst, load_sem.at[1 + i])
        for i, (src, dst) in enumerate(
            (
                (ret_hbm, ret_ref),
                (h_hbm, h_ref),
                (cot_hbm, tok_ref),
                (wout_hbm, wout_ref),
                (mixed_hbm, mixed_ref),
                (normed_hbm, qg_ref.at[:, :width]),
                (qkv_hbm, qkv_ref),
                (laug_hbm, laug_ref),
                (wqkv_hbm, wqkv_ref),
            )
        )
    ]
    for copy in loads[:5]:
        copy.start()
    load_tok = pltpu.make_async_copy(tok_hbm, tok_ref, load_sem.at[10])
    greet(experts, True)

    def send_ffn(r):
        share = experts // 16
        for j in range(r * share, (r + 1) * share):
            ffn_copy(experts // 2 + j).start()

    send_ffn(0)
    send_ffn(1)
    near_ffn.start()
    for copy in loads[5:]:
        copy.start()

    def core_copy(u, back):
        start, _, piece = plan[u]
        half = INNER * piece
        src = final if back else part
        mine, theirs = start + core * half, start + (1 - core) * half
        return pltpu.make_async_remote_copy(
            src_ref=src.at[rows(mine if back else theirs, half)],
            dst_ref=final.at[rows(mine, half)] if back else got_core.at[rows(start // 2, half)],
            send_sem=core_send.at[u, back], recv_sem=core_recv.at[u, back],
            device_id={"dp": 1 - core}, device_id_type=MESH,
        )

    def pair_copy(u, back):
        start, _, piece = plan[u]
        bit, side, _ = spot(u)
        base = start + core * INNER * piece
        own = final.at[rows(base + side * 4 * piece, 4 * piece)]
        return pltpu.make_async_remote_copy(
            src_ref=own if back else part.at[rows(base + (1 - side) * 4 * piece, 4 * piece)],
            dst_ref=own if back else got_pair.at[rows(start // 4, 4 * piece)],
            send_sem=pair_send.at[u, back], recv_sem=pair_recv.at[u, back],
            device_id={"expert": flip(me, 2**bit, experts)}, device_id_type=MESH,
        )

    def quad_copy(u, back, i):
        start, _, piece = plan[u]
        bit, side, place = spot(u)
        low, high = [b for b in range(3) if b != bit]
        base = start + (core * INNER + side * 4) * piece
        own = final.at[rows(base + place * piece, piece)]
        return pltpu.make_async_remote_copy(
            src_ref=own if back else part.at[rows(base + flip(place, i, 4) * piece, piece)],
            dst_ref=own if back else got_quad.at[i - 1, rows(start // (2 * INNER), piece)],
            send_sem=quad_send.at[u, back, i], recv_sem=quad_recv.at[u, back, i],
            device_id={"expert": flip(me, i % 2 * 2**low + i // 2 * 2**high, experts)}, device_id_type=MESH,
        )

    def outer_copy(u, i):
        start, _, piece = plan[u]
        own = got_out.at[far, rows(start // (2 * INNER), piece)]
        return pltpu.make_async_remote_copy(
            src_ref=own, dst_ref=own,
            send_sem=out_send.at[u, i], recv_sem=out_recv.at[u, i],
            device_id={"expert": flip(me, i * INNER, experts)}, device_id_type=MESH,
        )

    def add_up(to, sources, size):
        step = 16 * max(k for k in range(1, 13) if size // 16 % k == 0)

        @pl.loop(0, size // step)
        def _(n):
            r = rows_of(n, step)
            total = sources[0][r, :].astype(F32)
            for source in sources[1:]:
                total = total + source[r, :].astype(F32)
            to[r, :] = total.astype(BF)

    def advance(u, stage):
        start, _, piece = plan[u]
        half = INNER * piece
        _, side, place = spot(u)
        mine = part.at[rows(start + core * half, half)]
        quarter = part.at[rows(start + core * half + side * 4 * piece, 4 * piece)]
        at = rows(start + core * half + (side * 4 + place) * piece, piece)
        shared = rows(start // (2 * INNER), piece)
        if stage == 0:
            core_copy(u, 0).start()
        elif stage == 1:
            core_copy(u, 0).wait()
            add_up(mine, [mine, got_core.at[rows(start // 2, half)]], half)
            pair_copy(u, 0).start()
        elif stage == 2:
            pair_copy(u, 0).wait()
            add_up(quarter, [quarter, got_pair.at[rows(start // 4, 4 * piece)]], 4 * piece)
            for i in range(1, 4):
                quad_copy(u, 0, i).start()
        elif stage == 3:
            for i in range(1, 4):
                quad_copy(u, 0, i).wait()
            add_up(got_out.at[far, shared], [part.at[at]] + [got_quad.at[i, shared] for i in range(3)], piece)
            for i in range(1, outer):
                outer_copy(u, i).start()
        elif stage == 4:
            for i in range(1, outer):
                outer_copy(u, i).wait()
            add_up(final.at[at], [got_out.at[o, shared] for o in range(outer)], piece)
            for i in range(1, 4):
                quad_copy(u, 1, i).start()
        elif stage == 5:
            for i in range(1, 4):
                quad_copy(u, 1, i).wait()
            pair_copy(u, 1).start()
        elif stage == 6:
            pair_copy(u, 1).wait()
            core_copy(u, 1).start()
        else:
            core_copy(u, 1).wait()
            for copy in sums_copies(u):
                copy.start()

    def sums_copies(u):
        start, tiles, _ = plan[u]
        return [
            pltpu.make_async_copy(final.at[start + i * width : start + (i + 1) * width], sums_ref.at[tile], o_sem.at[tile])
            for i, tile in enumerate(tiles)
        ]

    for copy in loads[:5]:
        copy.wait()

    g2_acc[...] = jnp.zeros_like(g2_acc)

    @pl.loop(0, blocks)
    def _(i):
        r = rows_of(i)
        hat, inverse = normalize(h_ref[r, :])
        ing = collect(slot_col_ref, ret_ref, r)
        g2_acc[...] += jnp.sum((ing * hat).reshape(ROWS // 8, 8, width), axis=0)
        grad = tok_ref[r, :].astype(F32) + norm_back(ing * g2_ref[...].reshape(1, width), hat, inverse)
        hgrad_ref[r, :] = grad
        low = grad.astype(BF)
        hg_ref[r, :] = low
        mg = dot_t(low, wout_ref[...]).astype(BF)

        @pl.when(i == blocks // 2)
        def _():
            send_ffn(2)

        for p in range(pairs):
            piece = mg[:, p * LANES : (p + 1) * LANES]
            mg_ref[p, r, :] = piece
            prod = piece.astype(F32) * mixed_ref[r, p * LANES : (p + 1) * LANES].astype(F32)
            zero = jnp.zeros_like(prod)
            d0 = jnp.sum(jnp.where(first, prod, zero), axis=1, keepdims=True)
            d1 = jnp.sum(jnp.where(first, zero, prod), axis=1, keepdims=True)
            daug_ref[p, r, :] = aug_of(jnp.where(first, d1, d0), 0.0)

    load_tok.start()

    gain_at = len(plan[0][1]) * width
    spare = 2 * INNER * plan[0][2] - gain_at
    part[gain_at : gain_at + spare, :] = jnp.zeros((spare, LANES), BF)
    for p in range(pairs):
        gain = jnp.sum(g2_acc[:, p * LANES : (p + 1) * LANES], axis=0, keepdims=True)
        part[gain_at + 16 * p : gain_at + 16 * p + 1, :] = gain.astype(BF)

    @pl.loop(0, width // 256)
    def _(n):
        out = tdot(mixed_ref[...], hg_ref[:, rows_of(n, 256)]).astype(BF)
        for m in range(2):
            tile = 2 * n + m
            third = pairs // 3
            at = tile * width + jnp.where(tile < third, 0, spare)
            part[rows(at, width), :] = out[:, m * LANES : (m + 1) * LANES]

    send_ffn(3)
    for n in range(3):
        advance(n, 0)
    loads[5].wait()

    @pl.loop(0, blocks)
    def _(i):
        r = rows_of(i)
        normt_ref[:, r] = qg_ref[r, :width].T

    kaug_ref[...] = key_aug(seq, len_ref[0])
    scale = jnp.asarray(HEAD**-0.5, BF)
    for copy in loads[6:]:
        copy.wait()

    ends = {}
    for unit, points in enumerate(STAGES):
        for stage, at in enumerate(points):
            ends.setdefault(at, []).extend((3 * unit + n, stage) for n in range(3))

    @pl.loop(0, pairs)
    def _(p):
        keep = lane_iota((ROWS, ROWS)) >= lax.broadcasted_iota(I32, (ROWS, ROWS), 0)
        vaug = jnp.where(lane_iota((ROWS, LANES)) % HEAD < 3, 1.0, 0.0).astype(BF)
        none = jnp.zeros((ROWS, LANES), BF)
        dq_ref[...] = jnp.zeros_like(dq_ref)
        for j in range(blocks):
            kr = slice(j * ROWS, (j + 1) * ROWS)
            qr = slice(j * ROWS, seq)
            q = qkv_ref[p, qr, :] * scale
            k = qkv_ref[pairs + p, kr, :]
            v = qkv_ref[2 * pairs + p, kr, :]
            do = mg_ref[p, qr, :]
            la, da = laug_ref[p, qr, :], daug_ref[p, qr, :]
            ka = kaug_ref[kr, :]
            dvs, dks, dss, kms = [], [], [], []
            for head in range(2):
                mine = first if head == 0 else ~first
                s = dot_t(jnp.where(mine, k, ka), jnp.where(mine, q, la))
                e = jnp.exp(s)
                start = jnp.where(keep, e[:, :ROWS], 0.0)
                e = jnp.concatenate([start, e[:, ROWS:]], axis=1) if j < blocks - 1 else start
                dp = dot_t(jnp.where(mine, v, vaug), jnp.where(mine, do, da))
                ds = (e * dp).astype(BF)
                dvs.append(dot(e.astype(BF), do))
                dks.append(dot(ds, q))
                dss.append(ds)
                kms.append(jnp.where(mine, k, none))
            qg_ref[kr, rows_of(2 * pairs + p, LANES)] = jnp.where(first, dvs[0], dvs[1]).astype(BF)
            qg_ref[kr, rows_of(pairs + p, LANES)] = jnp.where(first, dks[0], dks[1]).astype(BF)
            dq_ref[qr, :] += tdot(jnp.concatenate(dss, axis=0), jnp.concatenate(kms, axis=0))
        qg_ref[:, rows_of(p, LANES)] = (dq_ref[...] * HEAD**-0.5).astype(BF)

        tiles3 = [qg_ref[:, rows_of(n * pairs + p, LANES)] for n in range(3)]
        out = dot(normt_ref[...], jnp.concatenate(tiles3, axis=1)).astype(BF)
        for n in range(3):
            early = p // 2 * 6 + n * 2 + p % 2
            at = plan[3][0] + jnp.where(p < pairs - 2, early, 3 * p + n) * width
            part[rows(at, width), :] = out[:, n * LANES : (n + 1) * LANES]

        for at in range(pairs):

            @pl.when(p == at)
            def _():
                if at < 4:
                    send_ffn(4 + at)
                for u, stage in ends.get(at, ()):
                    advance(u, stage)

    load_tok.wait()

    def finish_tokens(i):
        r = rows_of(i)
        n1 = dot_t(qg_ref[r, :], wqkv_ref[...])
        hat, inverse = normalize(tok_ref[r, :].astype(F32))
        hgrad_ref[r, :] = hgrad_ref[r, :] + norm_back(n1 * g1_ref[...].reshape(1, width), hat, inverse)
        tokg_copy(i).start()

    def tokg_copy(i):
        return pltpu.make_async_copy(hgrad_ref.at[rows_of(i)], tokg_ref.at[rows_of(i)], load_sem.at[1 + i])

    def finish_output(i):
        r = rows_of(i)
        h_ref[r, :] = h_ref[r, :] + collect(slot_col_ref, ffn_ref, r)
        out_copy(i).start()

    def out_copy(i):
        return pltpu.make_async_copy(h_ref.at[rows_of(i)], out_ref.at[rows_of(i)], load_sem.at[1 + blocks + i])

    for step in range(pairs, max(ends) + 1):
        for u, stage in ends[step]:
            advance(u, stage)
        n = step - pairs
        if n < blocks:
            finish_tokens(n)
        elif n < blocks + 2:
            if n == blocks:
                near_ffn.wait()

                @pl.loop(experts // 2, experts)
                def _(j):
                    ffn_copy(j).wait()

            for i in range((n - blocks) * blocks // 2, (n - blocks + 1) * blocks // 2):
                finish_output(i)

    for p in range(pairs):
        g2g_ref[p * LANES : (p + 1) * LANES] = final[gain_at + 16 * p : gain_at + 16 * p + 1, :].astype(F32).reshape(LANES)
    for i in range(blocks):
        tokg_copy(i).wait()
        out_copy(i).wait()
    for u in range(len(plan)):
        for copy in sums_copies(u):
            copy.wait()


def backward_call(experts, capacity, lengths, g1, g2, x, g, normed, qkv, mixed, laug, h, ret, slot_col, w_qkv, w_out, ffn, got):
    seq, width = x.shape
    pairs, total = width // LANES, experts * capacity
    plan, height = unit_plan(width)
    outer, units = experts // INNER, len(plan)
    dma = pltpu.SemaphoreType.DMA
    vmem = pltpu.VMEM
    return pl.pallas_call(
        functools.partial(backward_kernel, experts, capacity),
        out_shape=(
            sds((seq, width), F32), sds((seq, width), F32), sds((4 * pairs, width, LANES), BF), sds((width,), F32),
        ),
        in_specs=[SMEM, VMEM, VMEM] + [ANY] * 8 + [VMEM] + [ANY] * 4,
        out_specs=(ANY, ANY, ANY, VMEM),
        scratch_shapes=[
            vmem((seq, width), BF),
            vmem((3 * pairs, seq, LANES), BF),
            vmem((seq, width), BF),
            vmem((pairs, seq, LANES), BF),
            vmem((seq, width), F32),
            vmem((total, width), BF),
            vmem((width, 3 * width), BF),
            vmem((width, width), BF),
            vmem((total, width), BF),
            vmem((seq, width), F32),
            vmem((seq, width), BF),
            vmem((pairs, seq, LANES), BF),
            vmem((pairs, seq, LANES), BF),
            vmem((seq, LANES), BF),
            vmem((seq, LANES), F32),
            vmem((seq, 3 * width), BF),
            vmem((width, seq), BF),
            vmem((height, LANES), BF),
            vmem((height, LANES), BF),
            vmem((height // 2, LANES), BF),
            vmem((height // 4, LANES), BF),
            vmem((3, height // (2 * INNER), LANES), BF),
            vmem((outer, height // (2 * INNER), LANES), BF),
            vmem((8, width), F32),
            dma((11,)), dma((experts,)), dma((experts,)),
            dma((units, 2)), dma((units, 2)),
            dma((units, 2)), dma((units, 2)),
            dma((units, 2, 4)), dma((units, 2, 4)),
            dma((units, outer)), dma((units, outer)),
            dma((4 * pairs,)),
        ],
        compiler_params=params(62, collective_id=2, has_side_effects=True),
        cost_estimate=pl.CostEstimate(flops=60 * 10**9, bytes_accessed=24 * 10**6, transcendentals=0),
        name="attention_backward",
    )(lengths, g1, g2, x, g, normed, qkv, mixed, laug, h, ret, slot_col, w_qkv, w_out, ffn, got)


def finish_kernel(
    win_ref, wback_ref, sums_ref, wqkv_ref, g1_ref, out_ref, tokg_ref,
    win_out, wback_out, wqkv_out, wout_out, g1g_ref, out_out, tokg_out,
    gain_ref,
):
    i = pl.program_id(0)
    size = wqkv_ref.shape[0]
    tiles = sums_ref.shape[0]
    pairs = tiles // 4
    out_out[...] = out_ref[...]
    tokg_out[...] = tokg_ref[...]
    win_out[...] = win_ref[...].astype(F32)
    wback_out[...] = wback_ref[...].astype(F32)
    gain = jnp.zeros((size, LANES), F32)
    for t in range(tiles):
        tile = sums_ref[t].astype(F32)
        if t < 3 * pairs:
            c = slice(t * LANES, (t + 1) * LANES)
            wqkv_out[:, c] = tile
            gain = gain + tile * wqkv_ref[:, c].astype(F32)
        else:
            wout_out[:, (t - 3 * pairs) * LANES : (t - 3 * pairs + 1) * LANES] = tile
    gain_ref[rows_of(i, size), :] = gain

    @pl.when(i == pl.num_programs(0) - 1)
    def _():
        total = lax.dot_general(
            jnp.ones((8, LANES), F32), gain_ref[...], (((1,), (1,)), ((), ())),
            precision=lax.Precision.HIGHEST, preferred_element_type=F32,
        )
        g1g_ref[...] = (total[0] / g1_ref[...])


def finish_call(win, wback, sums, w_qkv, g1, out, tokg):
    width, ff = win.shape
    tiles, steps = sums.shape[0], 8
    wide = pl.BlockSpec((width // steps, ff), lambda i: (i, 0))
    tall = pl.BlockSpec((ff // steps, width), lambda i: (i, 0))
    three = pl.BlockSpec((width // steps, 3 * width), lambda i: (i, 0))
    square = pl.BlockSpec((width // steps, width), lambda i: (i, 0))
    row = pl.BlockSpec((width,), lambda i: (0,))
    part = pl.BlockSpec((out.shape[0] // steps, width), lambda i: (i, 0))
    return pl.pallas_call(
        finish_kernel,
        grid=(steps,),
        out_shape=(
            sds((width, ff), F32), sds((ff, width), F32), sds((width, 3 * width), F32), sds((width, width), F32),
            sds((width,), F32), sds(out.shape, F32), sds(out.shape, F32),
        ),
        in_specs=[wide, tall, pl.BlockSpec((tiles, width // steps, LANES), lambda i: (0, i, 0)), three, row, part, part],
        out_specs=(wide, tall, three, square, row, part, part),
        scratch_shapes=[pltpu.VMEM((width, LANES), F32)],
        compiler_params=params(61),
        name="finish_gradients",
    )(win, wback, sums, w_qkv, g1, out, tokg)


def params(mib, **kw):
    return pltpu.CompilerParams(vmem_limit_bytes=mib * MIB, **kw)


def sds(shape, dtype):
    return jax.ShapeDtypeStruct(shape, dtype)


def shards(experts, tokens, lengths, expert_ids, w_qkv, w_out, norm1_gain, norm2_gain, w_in, w_back, cotangent):
    x, g = tokens[0], cotangent[0]
    seq, width = x.shape
    pairs = width // LANES
    capacity = 3 * seq // (2 * experts)
    capacity = (capacity + 15) // 16 * 16
    total = experts * capacity
    eid_row = expert_ids.reshape(1, seq)
    g1, g2 = norm1_gain, norm2_gain

    normed, qkv, mixed, laug, h, x_slots, slot_col, g_in = forward_call(
        experts, capacity, lengths, eid_row, g1, g2, x, g, w_qkv, w_out
    )
    ing_ret, ffn, got, wing, wbg = experts_call(experts, capacity, x_slots, g_in, w_in[0], w_back[0])
    output, tokg, sums, g2_sum = backward_call(
        experts, capacity, lengths, g1, g2, x, g, normed, qkv, mixed, laug, h, ing_ret, slot_col, w_qkv, w_out, ffn, got
    )
    in_sum, back_sum, qkv_sum, out_sum, g1_sum, output, tokg = finish_call(wing, wbg, sums, w_qkv, g1, output, tokg)
    return (
        output[None], tokg[None], qkv_sum, out_sum, g1_sum, g2_sum, in_sum[None], back_sum[None],
    )


def solution(mesh):
    split = P(("dp", "expert"), None, None)
    mine = P("expert", None, None)
    return jax.shard_map(
        functools.partial(shards, mesh.shape["expert"]),
        mesh=mesh,
        in_specs=(split, P(("dp", "expert")), split, P(), P(), P(), P(), mine, mine, split),
        out_specs=(split, split, P(), P(), P(), P(), mine, mine),
        check_vma=False,
    )
```
